256 devices in a mesh: copy: 32 (over z, y_hi, core), table: 8 (over y_lo, x).
Axes of the slice: x: 4, y: 4 (y_hi: 2, y_lo: 2; y = y_hi * 2 + y_lo), z: 8, core: 2. Of those that a mesh axis runs over, the one named last changes fastest.
Arguments:
- pooled: bfloat16 [8192, 40, 128], P('copy', 'table'), may hold values from -6 to 6
- slot_of_table: int32 [26], replicated, may hold values from 0 to 39, as said below
- partner: int32 [32], replicated, may hold values from 0 to 31, as said below
- labels: int32 [8192], P('copy'), may hold values 0 or 1
- w_first: bfloat16 [32, 3328, 4096], P('copy', None, 'table'), may hold values from -0.109375 to 0.109375
- b_first: bfloat16 [32, 4096], P('copy', 'table'), may hold values from -3 to 3
- w_head: bfloat16 [32, 4096], P('copy', 'table'), may hold values from -0.1875 to 0.1875
Outputs:
- pooled_grad: bfloat16 [40, 128, 8192], P('table', None, 'copy')
- grad_first: bfloat16 [32, 3328, 4096], P('copy', None, 'table')
- grad_bias: float32 [32, 4096], P('copy', 'table')
- grad_head: float32 [32, 4096], P('copy', 'table')
- loss_mean: float32 [32], P('copy')
The draws below stay inside these ranges and needn't reach their ends.
Inputs may be any that keep to these rules, and one draw needn't show every extreme that they name: The slots are distinct; table t lies on the device of index slot_of_table[t] // 5 of the table axis; slots 0 and 39 are always used. A pairing: partner[partner[c]] == c and partner[c] != c.
All inputs are finite; a program needn't handle non-finite values. No bound on the sum of `labels` on one device may be relied on, other than what follows from the above.
Results may differ from the reference program's by a relative error of at most 0.017.
Values may be sent and summed in bfloat16 or wider, within the bound.
A program may use at most 64 MiB of HBM per device.

```python
import jax
import jax.numpy as jnp
from jax import lax

TABLES = 26
EMB = 128
H1 = 4096
GROUP_ROWS = 256
COPIES = 32
FEATURES = 3328
SLOTS = 40
ROWS = 8192
N_TABLE = 8


def draw_slot_of_table(key, part):
    key = jax.random.fold_in(key, 11)
    first_key, second_key = jax.random.split(key)
    middle = jax.random.permutation(first_key, jnp.arange(1, SLOTS - 1, dtype=jnp.int32))
    chosen = jnp.concatenate([jnp.array([0, SLOTS - 1], dtype=jnp.int32), middle[:TABLES - 2]])
    return jax.random.permutation(second_key, chosen)


def draw_partner(key, part):
    key = jax.random.fold_in(key, 23)
    ordering = jax.random.permutation(key, jnp.arange(COPIES, dtype=jnp.int32))
    positions = jnp.arange(COPIES, dtype=jnp.int32)
    mates = ordering[jnp.bitwise_xor(positions, 1)]
    return jnp.zeros((COPIES,), jnp.int32).at[ordering].set(mates)


def with_ends(result, own_key, least, top_value):
    longest = result.shape.index(max(result.shape))
    spots = []
    for shift in (0, 1):
        where = [jax.random.randint(jax.random.fold_in(own_key, axis), (), 0, length) for axis, length in enumerate(result.shape)]
        where[longest] = (where[longest] + shift) % result.shape[longest]
        spots.append(tuple(where))
    return result.at[spots[0]].set(least).at[spots[1]].set(top_value)


def steps_of(rng, extent, cuts, low, top_value):
    gain, own = 1.0, jax.random.fold_in(rng, 6)
    for dim, shards_of in cuts:
        steps = jnp.exp(jax.random.uniform(jax.random.fold_in(own, dim), (shards_of,), jnp.float32, low / len(cuts), top_value / len(cuts)))
        gain = gain * jnp.repeat(steps, extent[dim] // shards_of).reshape([-1 if axis == dim else 1 for axis in range(len(extent))])
    return gain


def centred(key, shape, width, reach, pieces=(), held_as=jnp.bfloat16):
    gain = steps_of(key, shape, pieces, -0.22, 0.18) if pieces else 1.0
    result = jax.random.normal(key, shape, jnp.float32) * width * gain
    return jnp.minimum(jnp.maximum(result, -reach), reach).astype(held_as)


def setup_inputs(seed: int = 0) -> dict:
    keys = jax.random.split(jax.random.key(seed), 8)
    return {
        "pooled": centred(keys[0], (ROWS, SLOTS, EMB), 1.0, 6.0, ((0, 32), (1, 8))),
        "slot_of_table": draw_slot_of_table(jax.random.fold_in(keys[7], 71), 0),
        "partner": draw_partner(jax.random.fold_in(keys[7], 71), 0),
        "labels": with_ends((jax.random.randint(keys[3], (ROWS,), 0, 4) < 1).astype(jnp.int32), jax.random.fold_in(keys[3], 1), 0, 1),
        "w_first": centred(keys[4], (COPIES, FEATURES, H1), FEATURES ** -0.5, 0.109375, ((0, 32), (2, 8))),
        "b_first": centred(keys[5], (COPIES, H1), 0.5, 3.0, ((0, 32), (1, 8))),
        "w_head": centred(keys[6], (COPIES, H1), (H1 // 4) ** -0.5, 0.1875, ((0, 32), (1, 8))),
    }


def swish_parts(pre_value):
    sigmoid_v = jax.nn.sigmoid(pre_value)
    return pre_value * sigmoid_v, sigmoid_v * (1.0 + pre_value * (1.0 - sigmoid_v))


def one_copy(pooled_copy, slot_of_table, labels_copy, w_own, b_own, h_own, w_peer, b_peer, h_peer):
    row_count = pooled_copy.shape[0]
    features = jnp.take(pooled_copy, slot_of_table, axis=1).reshape(row_count, -1)
    student_pre = jnp.dot(features, w_own, preferred_element_type=jnp.float32) + b_own.astype(jnp.float32)
    teacher_pre = jnp.dot(features, w_peer, preferred_element_type=jnp.float32) + b_peer.astype(jnp.float32)
    activation, derivative = swish_parts(student_pre)
    teacher_act, unused_slope = swish_parts(teacher_pre)
    student_logit = jnp.sum(activation * h_own.astype(jnp.float32)[None, :], axis=1)
    teacher_logit = jnp.sum(teacher_act * h_peer.astype(jnp.float32)[None, :], axis=1)
    targets = labels_copy.astype(jnp.float32)
    soft_target = jax.nn.sigmoid(teacher_logit)
    loss_mean = jnp.mean(2.0 * jax.nn.softplus(student_logit) - targets * student_logit - soft_target * student_logit)
    logit_grad = 2.0 * jax.nn.sigmoid(student_logit) - targets - soft_target
    grad_pre = logit_grad[:, None] * h_own.astype(jnp.float32)[None, :] * derivative
    grad_low = grad_pre.astype(jnp.bfloat16)
    grad_first = lax.dot_general(features, grad_low, (((0,), (0,)), ((), ())), preferred_element_type=jnp.float32).astype(jnp.bfloat16)
    grad_bias = jnp.sum(grad_pre, axis=0)
    grad_head = jnp.sum(logit_grad[:, None] * activation, axis=0)
    unit_width = w_own.shape[1] // N_TABLE
    summed = jnp.zeros((row_count, SLOTS, EMB), jnp.float32)
    for block_index in range(N_TABLE):
        lower = block_index * unit_width
        partial_value = lax.dot_general(grad_low[:, lower:lower + unit_width], w_own[:, lower:lower + unit_width], (((1,), (1,)), ((), ())), preferred_element_type=jnp.float32)
        partial_value = lax.optimization_barrier(partial_value.astype(jnp.bfloat16)).astype(jnp.float32)
        placed = jnp.zeros((row_count, SLOTS, EMB), jnp.float32).at[:, slot_of_table, :].add(partial_value.reshape(row_count, TABLES, EMB))
        summed = summed + placed
    pooled_grad = jnp.transpose(summed, (1, 2, 0)).astype(jnp.bfloat16)
    return pooled_grad, grad_first, grad_bias, grad_head, loss_mean


def reference(pooled, slot_of_table, partner, labels, w_first, b_first, w_head):
    pooled_copies = pooled.reshape(COPIES, GROUP_ROWS, SLOTS, EMB)
    label_copies = labels.reshape(COPIES, GROUP_ROWS)

    def per_copy(copy_index):
        peer_index = partner[copy_index]
        return one_copy(pooled_copies[copy_index], slot_of_table, label_copies[copy_index], w_first[copy_index], b_first[copy_index], w_head[copy_index], w_first[peer_index], b_first[peer_index], w_head[peer_index])

    results = lax.map(per_copy, jnp.arange(COPIES, dtype=jnp.int32))
    pooled_grad = jnp.transpose(results[0], (1, 2, 0, 3)).reshape(SLOTS, EMB, ROWS)
    return pooled_grad, results[1], results[2], results[3], results[4]
```

```python
import jax
import jax.numpy as jnp
from jax import lax
from jax.experimental import pallas as pl
from jax.experimental.pallas import tpu as pltpu
from jax.sharding import PartitionSpec as P

MESH = pl.DeviceIdType.MESH
F32, BF16 = jnp.float32, jnp.bfloat16
NT, NC = 8, 32
TAB, EMB, SLOTS, LOCAL = 26, 128, 40, 5
ROWS, HID, FEAT = 256, 512, 3328
RB = ROWS // NT
EB = EMB // NT
CH = 256
NCHUNK = FEAT // CH


def relay_copy(t):
    return jnp.where(t < 24, (t // 3) * 4 + t % 3, jnp.where(t == 24, 3, 19))


def kernel(
    slot_s, partner_s, inv_s, labels_v, pooled, w_hbm, b_v, h_v,
    pg_out, gf_out, gb_out, gh_out, loss_out,
    w_v, feat, feat_t, by_slot, relay_in, relay_out, act_v, a32_v, low_v, gt_v, part_in, sums, placed,
    gf_v, lg_own, lg_in, tl_own, tl_in,
    w_sem, gf_sem,
    a_send, a_recv, ag_send, ag_recv, c_send, c_recv, d_send, d_recv, tg_send, tg_recv,
    l_send, l_recv, t_send, t_recv, r_send, r_recv, z_send, z_recv,
):
    c = lax.axis_index("copy")
    k = lax.axis_index("table")
    my_rows = pl.ds(pl.multiple_of(k * RB, RB), RB)
    zq = lax.rem(c, 4)
    my_t = jnp.where(zq < 3, (c // 4) * 3 + zq, jnp.where(c == 3, 24, 25))
    is_relay = jnp.logical_or(zq < 3, jnp.logical_or(c == 3, c == 19))

    w_copy = pltpu.make_async_copy(w_hbm, w_v, w_sem)
    w_copy.start()

    barrier = pltpu.get_barrier_semaphore()

    def greet_table(d, _):
        pl.semaphore_signal(barrier, inc=1, device_id=(c, lax.rem(k + d, NT)), device_id_type=MESH)
        return 0

    def greet_copy(d, _):
        pl.semaphore_signal(barrier, inc=1, device_id=(lax.rem(c + d, NC), k), device_id_type=MESH)
        return 0

    lax.fori_loop(1, NT, greet_table, 0)
    lax.fori_loop(1, NC, greet_copy, 0)
    pl.semaphore_wait(barrier, NT - 1 + NC - 1)

    def remote(src, dst, send, recv, copy, table):
        return pltpu.make_async_remote_copy(
            src_ref=src, dst_ref=dst, send_sem=send, recv_sem=recv, device_id=(copy, table), device_id_type=MESH
        )

    def over_table(fn):
        def body(d, _):
            fn(d, lax.rem(k + d, NT))
            return 0

        lax.fori_loop(1, NT, body, 0)

    def take(ref, sem):
        pltpu.make_async_copy(ref, ref, sem).wait()

    def a_copy(d, j):
        rows = pl.ds(pl.multiple_of(j * RB, RB), RB)
        return remote(pooled.at[:, rows, :], by_slot.at[pl.ds(k * LOCAL, LOCAL)], a_send.at[d], a_recv, c, j)

    over_table(lambda d, j: a_copy(d, j).start())
    pltpu.make_async_copy(pooled.at[:, my_rows, :], by_slot.at[pl.ds(k * LOCAL, LOCAL)], a_recv).start()
    take(by_slot, a_recv)
    for t in range(TAB):
        feat[my_rows, t * EMB : (t + 1) * EMB] = by_slot[slot_s[t]]

    def c_copy(i):
        t = lax.rem(i + my_t, TAB)
        target = relay_copy(t)
        src = feat.at[my_rows, pl.ds(pl.multiple_of(t * EMB, EMB), EMB)]
        return src, target, remote(src, relay_in.at[c], c_send.at[i], c_recv, target, k)

    def c_start(i, _):
        src, target, copy = c_copy(i)

        @pl.when(target != c)
        def _():
            copy.start()

        @pl.when(target == c)
        def _():
            pltpu.make_async_copy(src, relay_in.at[c], c_recv).start()

        return 0

    lax.fori_loop(0, TAB, c_start, 0)

    def ag_copy(buf, send, recv, d, j):
        return remote(buf.at[my_rows], buf.at[my_rows], send.at[d], recv.at[k], c, j)

    over_table(lambda d, j: ag_copy(feat, ag_send, ag_recv, d, j).start())

    def d_copy(d, p):
        t = pl.ds(pl.multiple_of(my_t * EMB, EMB), EMB)
        return remote(relay_out.at[p], feat_t.at[my_rows, t], d_send.at[d], d_recv, p, k)

    @pl.when(is_relay)
    def _():
        take(relay_in, c_recv)

        def pick(p, _):
            relay_out[p] = relay_in[partner_s[p]]
            return 0

        lax.fori_loop(0, NC, pick, 0, unroll=4)

        def d_start(d, _):
            d_copy(d, lax.rem(c + d, NC)).start()
            return 0

        lax.fori_loop(1, NC, d_start, 0)
        t = pl.ds(pl.multiple_of(my_t * EMB, EMB), EMB)
        pltpu.make_async_copy(relay_out.at[c], feat_t.at[my_rows, t], d_recv).start()

    take(feat_t.at[my_rows], d_recv)
    over_table(lambda d, j: ag_copy(feat_t, tg_send, tg_recv, d, j).start())

    def ag_wait(buf, send, recv):
        def body(d, j):
            rows = pl.ds(pl.multiple_of(j * RB, RB), RB)
            take(buf.at[rows], recv.at[j])

        over_table(body)

    def head_row(total):
        return jnp.sum(jnp.transpose(total), axis=0, keepdims=True)

    ag_wait(feat, ag_send, ag_recv)
    w_copy.wait()
    total = jnp.zeros((ROWS, EMB), F32)
    for n in range(HID // CH):
        cols = slice(n * CH, (n + 1) * CH)
        head = h_v[:, cols].astype(F32)
        pre = jnp.dot(feat[...], w_v[:, cols], preferred_element_type=F32) + b_v[:, cols].astype(F32)
        sig = jax.nn.sigmoid(pre)
        act = pre * sig
        act_v[:, cols] = act
        a32 = head * (sig * (1.0 + pre * (1.0 - sig)))
        a32_v[:, cols] = a32
        low_v[:, cols] = a32.astype(BF16)
        weighed = act * head
        total = total + (weighed[:, :EMB] + weighed[:, EMB:])
    lg_own[...] = jnp.zeros_like(lg_own)
    lg_own[0:1, :] = head_row(total)

    def gt_step(i, _):
        rows = pl.ds(pl.multiple_of(i * CH, CH), CH)
        g = lax.dot_general(w_v[rows, :], low_v[...], (((1,), (1,)), ((), ())), preferred_element_type=F32)
        gt_v[pl.ds(i * 2, 2)] = g.astype(BF16).reshape(2, EMB, ROWS)
        return 0

    lax.fori_loop(0, NCHUNK, gt_step, 0)

    def r_copy(d, j):
        part = pl.ds(pl.multiple_of(j * EB, EB), EB)
        return remote(gt_v.at[:, part, :], part_in.at[k], r_send.at[d], r_recv, c, j)

    over_table(lambda d, j: r_copy(d, j).start())
    my_part = pl.ds(pl.multiple_of(k * EB, EB), EB)
    pltpu.make_async_copy(gt_v.at[:, my_part, :], part_in.at[k], r_recv).start()

    ag_wait(feat_t, tg_send, tg_recv)
    total = jnp.zeros((ROWS, EMB), F32)
    for n in range(HID // CH):
        cols = slice(n * CH, (n + 1) * CH)
        pre = jnp.dot(feat_t[...], w_v[:, cols], preferred_element_type=F32) + b_v[:, cols].astype(F32)
        weighed = pre * jax.nn.sigmoid(pre) * h_v[:, cols].astype(F32)
        total = total + (weighed[:, :EMB] + weighed[:, EMB:])
    lg_own[1:2, :] = head_row(total)

    lg_in[k] = lg_own[...]

    def l_copy(d, j):
        return remote(lg_own, lg_in.at[k], l_send.at[d], l_recv, c, j)

    over_table(lambda d, j: l_copy(d, j).start())
    take(lg_in.at[pl.ds(0, NT - 1)], l_recv)
    tl_own[...] = jnp.sum(lg_in[...], axis=0)
    tl_in[c] = tl_own[...]

    def t_copy(d):
        return remote(tl_own, tl_in.at[c], t_send.at[d], t_recv, lax.rem(c + d, NC), k)

    def t_start(d, _):
        t_copy(d).start()
        return 0

    lax.fori_loop(1, NC, t_start, 0)
    take(tl_in.at[pl.ds(0, NC - 1)], t_recv)

    z = tl_own[0:1, :]
    q = jax.nn.sigmoid(tl_in[partner_s[c]][1:2, :])
    y = labels_v[...].astype(F32)
    soft = jnp.maximum(z, 0.0) + jnp.log1p(jnp.exp(-jnp.abs(z)))
    loss_out[0] = jnp.sum(2.0 * soft - y * z - q * z) * (1.0 / ROWS)
    lg = 2.0 * jax.nn.sigmoid(z) - y - q
    lg_col = jnp.transpose(jnp.broadcast_to(lg, (EMB, ROWS)))
    for n in range(HID // EMB):
        cols = slice(n * EMB, (n + 1) * EMB)
        grad_pre = lg_col * a32_v[:, cols]
        low_v[:, cols] = grad_pre.astype(BF16)
        gb_out[:, cols] = jnp.sum(grad_pre, axis=0, keepdims=True)
        gh_out[:, cols] = jnp.sum(lg_col * act_v[:, cols], axis=0, keepdims=True)

    def gf_copy(i):
        rows = pl.ds(pl.multiple_of(i * CH, CH), CH)
        return pltpu.make_async_copy(gf_v.at[rows], gf_out.at[rows], gf_sem.at[i])

    def gf_step(i, _):
        rows = pl.ds(pl.multiple_of(i * CH, CH), CH)
        g = lax.dot_general(feat[:, rows], low_v[...], (((0,), (0,)), ((), ())), preferred_element_type=F32)
        gf_v[rows, :] = g.astype(BF16)
        gf_copy(i).start()
        return 0

    lax.fori_loop(0, NCHUNK, gf_step, 0)

    take(part_in, r_recv)
    sums[TAB] = jnp.zeros((EB, ROWS), BF16)

    def sum_step(t, _):
        total = part_in[0, t].astype(F32)
        for j in range(1, NT):
            total = total + part_in[j, t].astype(F32)
        sums[t] = (total * lg).astype(BF16)
        return 0

    lax.fori_loop(0, TAB, sum_step, 0, unroll=2)

    def place(s, _):
        placed[s] = sums[inv_s[s]]
        return 0

    lax.fori_loop(0, SLOTS, place, 0, unroll=4)

    def z_copy(d, j):
        return remote(placed.at[pl.ds(j * LOCAL, LOCAL)], pg_out.at[:, my_part, :], z_send.at[d], z_recv, c, j)

    over_table(lambda d, j: z_copy(d, j).start())
    pltpu.make_async_copy(placed.at[pl.ds(k * LOCAL, LOCAL)], pg_out.at[:, my_part, :], z_recv).start()
    take(pg_out, z_recv)

    over_table(lambda d, j: a_copy(d, j).wait_send())

    def c_wait(i, _):
        _, target, copy = c_copy(i)

        @pl.when(target != c)
        def _():
            copy.wait_send()

        return 0

    lax.fori_loop(0, TAB, c_wait, 0)
    over_table(lambda d, j: ag_copy(feat, ag_send, ag_recv, d, j).wait_send())

    @pl.when(is_relay)
    def _():
        def d_wait(d, _):
            d_copy(d, lax.rem(c + d, NC)).wait_send()
            return 0

        lax.fori_loop(1, NC, d_wait, 0)

    over_table(lambda d, j: ag_copy(feat_t, tg_send, tg_recv, d, j).wait_send())
    over_table(lambda d, j: l_copy(d, j).wait_send())

    def t_wait(d, _):
        t_copy(d).wait_send()
        return 0

    lax.fori_loop(1, NC, t_wait, 0)
    over_table(lambda d, j: r_copy(d, j).wait_send())
    over_table(lambda d, j: z_copy(d, j).wait_send())

    def gf_wait(i, _):
        gf_copy(i).wait()
        return 0

    lax.fori_loop(0, NCHUNK, gf_wait, 0)


def on_device(pooled, slot_of_table, partner, labels, w_first, b_first, w_head):
    slots = jnp.arange(SLOTS, dtype=jnp.int32)[:, None]
    inverse = jnp.min(
        jnp.where(slots == slot_of_table[None, :], jnp.arange(TAB, dtype=jnp.int32)[None, :], TAB), axis=1
    )
    vmem = pl.BlockSpec(memory_space=pltpu.VMEM)
    smem = pl.BlockSpec(memory_space=pltpu.SMEM)
    hbm = pl.BlockSpec(memory_space=pl.ANY)
    dma = pltpu.SemaphoreType.DMA
    pg, gf, gb, gh, loss = pl.pallas_call(
        kernel,
        out_shape=(
            jax.ShapeDtypeStruct((LOCAL, EMB, ROWS), BF16),
            jax.ShapeDtypeStruct((FEAT, HID), BF16),
            jax.ShapeDtypeStruct((1, HID), F32),
            jax.ShapeDtypeStruct((1, HID), F32),
            jax.ShapeDtypeStruct((1,), F32),
        ),
        in_specs=[smem, smem, smem, vmem, hbm, hbm, vmem, vmem],
        out_specs=(vmem, hbm, vmem, vmem, smem),
        scratch_shapes=[
            pltpu.VMEM((FEAT, HID), BF16),
            pltpu.VMEM((ROWS, FEAT), BF16),
            pltpu.VMEM((ROWS, FEAT), BF16),
            pltpu.VMEM((SLOTS, RB, EMB), BF16),
            pltpu.VMEM((NC, RB, EMB), BF16),
            pltpu.VMEM((NC, RB, EMB), BF16),
            pltpu.VMEM((ROWS, HID), F32),
            pltpu.VMEM((ROWS, HID), F32),
            pltpu.VMEM((ROWS, HID), BF16),
            pltpu.VMEM((TAB, EMB, ROWS), BF16),
            pltpu.VMEM((NT, TAB, EB, ROWS), BF16),
            pltpu.VMEM((TAB + 1, EB, ROWS), BF16),
            pltpu.VMEM((SLOTS, EB, ROWS), BF16),
            pltpu.VMEM((FEAT, HID), BF16),
            pltpu.VMEM((8, ROWS), F32),
            pltpu.VMEM((NT, 8, ROWS), F32),
            pltpu.VMEM((8, ROWS), F32),
            pltpu.VMEM((NC, 8, ROWS), F32),
            dma, dma((NCHUNK,)),
            dma((NT,)), dma,
            dma((NT,)), dma((NT,)),
            dma((TAB,)), dma,
            dma((NC,)), dma,
            dma((NT,)), dma((NT,)),
            dma((NT,)), dma,
            dma((NC,)), dma,
            dma((NT,)), dma,
            dma((NT,)), dma,
        ],
        compiler_params=pltpu.CompilerParams(
            collective_id=0, has_side_effects=True, vmem_limit_bytes=48 * 1024 * 1024
        ),
    )(
        slot_of_table, partner, inverse, labels.reshape(1, ROWS), jnp.transpose(pooled, (1, 0, 2)),
        w_first.reshape(FEAT, HID), b_first, w_head,
    )
    return pg, gf[None], gb, gh, loss


def solution(mesh):
    in_specs = (
        P("copy", "table", None), P(), P(), P("copy"), P("copy", None, "table"), P("copy", "table"), P("copy", "table"),
    )
    out_specs = (
        P("table", None, "copy"), P("copy", None, "table"), P("copy", "table"), P("copy", "table"), P("copy"),
    )
    return jax.shard_map(on_device, mesh=mesh, in_specs=in_specs, out_specs=out_specs, check_vma=False)
```

```python
import jax
import jax.numpy as jnp
from jax import lax
from jax.experimental import pallas as pl
from jax.experimental.pallas import tpu as pltpu
from jax.sharding import PartitionSpec as P

MESH = pl.DeviceIdType.MESH
F32, BF16 = jnp.float32, jnp.bfloat16
NT, NC = 8, 32
TAB, EMB, SLOTS, LOCAL = 26, 128, 40, 5
ROWS, HID, FEAT = 256, 512, 3328
RB = ROWS // NT
EB = EMB // NT
CH = 256
NCHUNK = FEAT // CH
HALF = FEAT // 2

A, B, BOTH = (0, RB // 2), (RB // 2, RB // 2), (0, RB)
ALL, LOW, HIGH = (0, FEAT), (0, HALF), (HALF, HALF)
TREE = (
    ((0, 0), (0, 1), A, ALL, "y"),
    ((0, 0), (0, 1), B, ALL, "y"),
    ((0, 0), (3, 0), BOTH, ALL, "right"),
    ((0, 0), (1, 0), BOTH, ALL, "left"),
    ((0, 1), (3, 1), A, ALL, "right"),
    ((0, 1), (1, 1), A, ALL, "left"),
    ((3, 0), (2, 0), BOTH, LOW, "right"),
    ((1, 0), (2, 0), BOTH, HIGH, "left"),
    ((3, 0), (3, 1), B, ALL, "y"),
    ((1, 0), (1, 1), B, ALL, "y"),
    ((3, 1), (2, 1), A, LOW, "right"),
    ((1, 1), (2, 1), A, HIGH, "left"),
    ((2, 0), (2, 1), B, ALL, "y"),
)
TREE_STEPS = (((), (0, 2, 3, 1)), ((0,), (4, 5)), ((2,), (6, 8)), ((3,), (7, 9)), ((4,), (10,)), ((5,), (11,)), ((6, 7), (12,)),
              ((1, 8, 9, 10, 11, 12), ()))


def relay_copy(t):
    return jnp.where(t < 24, (t // 3) * 4 + t % 3, jnp.where(t == 24, 3, 19))


def kernel(
    slot_h, partner_h, labels_h, pooled, w_hbm, b_h, h_h,
    feat, act_v, a32_v, lg_out, pg_out,
    w_v, feat_t, by_slot, relay_in, relay_out, low_v, gt_v, part_in, sums, placed,
    z_own, z_in, q_own, q_in, qs_own, qs_in, b_v, h_v, y_v, slot_s, partner_s, inv_v, inv_s,
    load_sem, inv_sem,
    a_send, a_recv, ag_send, ag_recv, c_send, c_recv, d_send, d_recv, tg_send, tg_recv,
    l_send, l_recv, m_send, m_recv, t_send, t_recv, r_send, r_recv, z_send, z_recv,
):
    c = lax.axis_index("copy")
    k = lax.axis_index("table")
    x, y = lax.rem(k, 4), k // 4
    my_rows = pl.ds(pl.multiple_of(k * RB, RB), RB)
    zq = lax.rem(c, 4)
    my_t = jnp.where(zq < 3, (c // 4) * 3 + zq, jnp.where(c == 3, 24, 25))
    is_relay = jnp.logical_or(zq < 3, jnp.logical_or(c == 3, c == 19))

    barrier = pltpu.get_barrier_semaphore()

    def greet_table(d, _):
        pl.semaphore_signal(barrier, inc=1, device_id=(c, lax.rem(k + d, NT)), device_id_type=MESH)
        return 0

    def greet_copy(d, _):
        pl.semaphore_signal(barrier, inc=1, device_id=(lax.rem(c + d, NC), k), device_id_type=MESH)
        return 0

    lax.fori_loop(1, NT, greet_table, 0)
    lax.fori_loop(1, NC, greet_copy, 0)

    loads = [
        pltpu.make_async_copy(src, dst, load_sem.at[i])
        for i, (src, dst) in enumerate(
            ((slot_h, slot_s), (partner_h, partner_s), (labels_h, y_v), (b_h, b_v), (h_h, h_v), (w_hbm, w_v))
        )
    ]
    for load in loads:
        load.start()
    pl.semaphore_wait(barrier, NT - 1 + NC - 1)

    def remote(src, dst, send, recv, copy, table):
        return pltpu.make_async_remote_copy(
            src_ref=src, dst_ref=dst, send_sem=send, recv_sem=recv, device_id=(copy, table), device_id_type=MESH
        )

    def over_table(fn):
        def body(d, _):
            fn(d, lax.rem(k + d, NT))
            return 0

        lax.fori_loop(1, NT, body, 0)

    def take(ref, sem):
        pltpu.make_async_copy(ref, ref, sem).wait()

    def share(step):
        return lax.rem(y + step[1], 2) * 4 + lax.rem(x + step[0], 4)

    target = {"y": share((0, 1)), "right": share((1, 0)), "left": share((3, 0))}

    def region(buf, origin, rows, cols):
        first = pl.multiple_of(share(origin) * RB + rows[0], RB // 2)
        return buf.at[pl.ds(first, rows[1]), pl.ds(cols[0], cols[1])]

    def tree_copy(buf, send, recv, i):
        origin, _, rows, cols, to = TREE[i]
        piece = region(buf, origin, rows, cols)
        return remote(piece, piece, send.at[i], recv.at[i], c, target[to])

    def tree_step(buf, send, recv, step):
        waits, starts = TREE_STEPS[step]
        for i in waits:
            _, origin, rows, cols, _ = TREE[i]
            take(region(buf, origin, rows, cols), recv.at[i])
        for i in starts:
            tree_copy(buf, send, recv, i).start()

    def a_copy(d, j):
        rows = pl.ds(pl.multiple_of(j * RB, RB), RB)
        return remote(pooled.at[:, rows, :], by_slot.at[pl.ds(k * LOCAL, LOCAL)], a_send.at[d], a_recv, c, j)

    over_table(lambda d, j: a_copy(d, j).start())
    pltpu.make_async_copy(pooled.at[:, my_rows, :], by_slot.at[pl.ds(k * LOCAL, LOCAL)], a_recv).start()
    for load in loads:
        load.wait()

    lane = lax.broadcasted_iota(jnp.int32, (8, EMB), 1)
    slots = jnp.full((8, EMB), SLOTS, jnp.int32)
    for t in range(TAB):
        slots = jnp.where(lane == t, slot_s[t], slots)
    for i in range(SLOTS // 8):
        found = jnp.where(lax.broadcasted_iota(jnp.int32, (8, EMB), 0) + 8 * i == slots, lane, TAB)
        inv_v[8 * i : 8 * i + 8, :] = jnp.broadcast_to(jnp.min(found, axis=1, keepdims=True), (8, EMB))
    inv_copy = pltpu.make_async_copy(inv_v, inv_s, inv_sem)
    inv_copy.start()

    take(by_slot, a_recv)
    for t in range(TAB):
        feat[my_rows, t * EMB : (t + 1) * EMB] = by_slot[slot_s[t]]

    tree_step(feat, ag_send, ag_recv, 0)

    def c_copy(i):
        t = lax.rem(i + my_t, TAB)
        to = relay_copy(t)
        src = feat.at[my_rows, pl.ds(pl.multiple_of(t * EMB, EMB), EMB)]
        return src, to, remote(src, relay_in.at[c], c_send.at[i], c_recv, to, k)

    def c_start(i, _):
        src, to, copy = c_copy(i)

        @pl.when(to != c)
        def _():
            copy.start()

        @pl.when(to == c)
        def _():
            pltpu.make_async_copy(src, relay_in.at[c], c_recv).start()

        return 0

    lax.fori_loop(0, TAB, c_start, 0)
    for step in range(1, 6):
        tree_step(feat, ag_send, ag_recv, step)

    my_cols = pl.ds(pl.multiple_of(my_t * EMB, EMB), EMB)

    def d_copy(d, p):
        return remote(relay_out.at[p], feat_t.at[my_rows, my_cols], d_send.at[d], d_recv, p, k)

    @pl.when(is_relay)
    def _():
        take(relay_in, c_recv)

        def pick(p, _):
            relay_out[p] = relay_in[partner_s[p]]
            return 0

        lax.fori_loop(0, NC, pick, 0, unroll=4)

        def d_start(d, _):
            d_copy(d, lax.rem(c + d, NC)).start()
            return 0

        lax.fori_loop(1, NC, d_start, 0)
        pltpu.make_async_copy(relay_out.at[c], feat_t.at[my_rows, my_cols], d_recv).start()

    for step in range(6, len(TREE_STEPS)):
        tree_step(feat, ag_send, ag_recv, step)

    def head_row(total):
        return jnp.sum(jnp.transpose(total), axis=0, keepdims=True)

    total = jnp.zeros((ROWS, EMB), F32)
    for n in range(HID // CH):
        cols = slice(n * CH, (n + 1) * CH)
        head = h_v[:, cols].astype(F32)
        pre = jnp.dot(feat[...], w_v[:, cols], preferred_element_type=F32) + b_v[:, cols].astype(F32)
        sig = jax.nn.sigmoid(pre)
        act = pre * sig
        act_v[:, cols] = act
        a32 = head * (sig * (1.0 + pre * (1.0 - sig)))
        a32_v[:, cols] = a32
        low_v[:, cols] = a32.astype(BF16)
        weighed = act * head
        total = total + (weighed[:, :EMB] + weighed[:, EMB:])
    z_own[...] = head_row(total)

    def gt_step(i, _):
        rows = pl.ds(pl.multiple_of(i * CH, CH), CH)
        g = lax.dot_general(w_v[rows, :], low_v[...], (((1,), (1,)), ((), ())), preferred_element_type=F32)
        gt_v[pl.ds(i * 2, 2)] = g.astype(BF16).reshape(2, EMB, ROWS)
        return 0

    lax.fori_loop(0, NCHUNK, gt_step, 0)

    z_in[k] = z_own[...]

    def l_copy(d, j):
        return remote(z_own, z_in.at[k], l_send.at[d], l_recv, c, j)

    over_table(lambda d, j: l_copy(d, j).start())

    def r_copy(d, j):
        part = pl.ds(pl.multiple_of(j * EB, EB), EB)
        return remote(gt_v.at[:, part, :], part_in.at[k], r_send.at[d], r_recv, c, j)

    over_table(lambda d, j: r_copy(d, j).start())
    my_part = pl.ds(pl.multiple_of(k * EB, EB), EB)
    pltpu.make_async_copy(gt_v.at[:, my_part, :], part_in.at[k], r_recv).start()

    take(feat_t.at[my_rows], d_recv)
    tree_step(feat_t, tg_send, tg_recv, 0)

    take(part_in, r_recv)
    inv_copy.wait()
    sums[TAB] = jnp.zeros((EB, ROWS), BF16)

    def sum_step(t, _):
        total = part_in[0, t].astype(F32)
        for j in range(1, NT):
            total = total + part_in[j, t].astype(F32)
        sums[t] = total.astype(BF16)
        return 0

    lax.fori_loop(0, TAB, sum_step, 0, unroll=2)

    def place(s, _):
        placed[s] = sums[inv_s[s, 0]]
        return 0

    lax.fori_loop(0, SLOTS, place, 0, unroll=4)

    def z_copy(d, j):
        return remote(placed.at[pl.ds(j * LOCAL, LOCAL)], pg_out.at[:, my_part, :], z_send.at[d], z_recv, c, j)

    over_table(lambda d, j: z_copy(d, j).start())
    pltpu.make_async_copy(placed.at[pl.ds(k * LOCAL, LOCAL)], pg_out.at[:, my_part, :], z_recv).start()

    for step in range(1, len(TREE_STEPS)):
        tree_step(feat_t, tg_send, tg_recv, step)
    total = jnp.zeros((ROWS, EMB), F32)
    for n in range(HID // CH):
        cols = slice(n * CH, (n + 1) * CH)
        pre = jnp.dot(feat_t[...], w_v[:, cols], preferred_element_type=F32) + b_v[:, cols].astype(F32)
        weighed = pre * jax.nn.sigmoid(pre) * h_v[:, cols].astype(F32)
        total = total + (weighed[:, :EMB] + weighed[:, EMB:])
    q_own[...] = head_row(total)
    q_in[k] = q_own[...]

    def m_copy(d, j):
        return remote(q_own, q_in.at[k], m_send.at[d], m_recv, c, j)

    over_table(lambda d, j: m_copy(d, j).start())
    take(z_in.at[pl.ds(0, NT - 1)], l_recv)
    take(q_in.at[pl.ds(0, NT - 1)], m_recv)
    qs_own[...] = jnp.sum(q_in[...], axis=0)
    qs_in[c] = qs_own[...]

    def t_copy(d):
        return remote(qs_own, qs_in.at[c], t_send.at[d], t_recv, lax.rem(c + d, NC), k)

    def t_start(d, _):
        t_copy(d).start()
        return 0

    lax.fori_loop(1, NC, t_start, 0)
    take(qs_in.at[pl.ds(0, NC - 1)], t_recv)

    z = jnp.sum(z_in[...], axis=0)
    q = jax.nn.sigmoid(qs_in[partner_s[c]])
    target_y = y_v[...].astype(F32)
    soft = jnp.maximum(z, 0.0) + jnp.log1p(jnp.exp(-jnp.abs(z)))
    lg_out[...] = jnp.zeros_like(lg_out)
    lg_out[0:1, :] = 2.0 * jax.nn.sigmoid(z) - target_y - q
    lg_out[1:2, :] = 2.0 * soft - target_y * z - q * z

    take(pg_out, z_recv)

    over_table(lambda d, j: a_copy(d, j).wait_send())

    def c_wait(i, _):
        _, to, copy = c_copy(i)

        @pl.when(to != c)
        def _():
            copy.wait_send()

        return 0

    lax.fori_loop(0, TAB, c_wait, 0)
    for i in range(len(TREE)):
        tree_copy(feat, ag_send, ag_recv, i).wait_send()
        tree_copy(feat_t, tg_send, tg_recv, i).wait_send()

    @pl.when(is_relay)
    def _():
        def d_wait(d, _):
            d_copy(d, lax.rem(c + d, NC)).wait_send()
            return 0

        lax.fori_loop(1, NC, d_wait, 0)

    def t_wait(d, _):
        t_copy(d).wait_send()
        return 0

    lax.fori_loop(1, NC, t_wait, 0)

    def rest(d, j):
        l_copy(d, j).wait_send()
        m_copy(d, j).wait_send()
        r_copy(d, j).wait_send()
        z_copy(d, j).wait_send()

    over_table(rest)


def finish(feat, act_v, a32_v, lg_v, pg_v, pg_out, gf_out, gb_out, gh_out, loss_out, low_v, gf_v, gf_sem):
    lg = lg_v[0:1, :]
    lg_col = jnp.transpose(jnp.broadcast_to(lg, (EMB, ROWS)))
    for n in range(HID // EMB):
        cols = slice(n * EMB, (n + 1) * EMB)
        grad_pre = lg_col * a32_v[:, cols]
        low_v[:, cols] = grad_pre.astype(BF16)
        gb_out[:, cols] = jnp.sum(grad_pre, axis=0, keepdims=True)
        gh_out[:, cols] = jnp.sum(lg_col * act_v[:, cols], axis=0, keepdims=True)

    def gf_copy(i):
        rows = pl.ds(pl.multiple_of(i * CH, CH), CH)
        return pltpu.make_async_copy(gf_v.at[rows], gf_out.at[rows], gf_sem.at[i])

    def gf_step(i, _):
        rows = pl.ds(pl.multiple_of(i * CH, CH), CH)
        g = lax.dot_general(feat[:, rows], low_v[...], (((0,), (0,)), ((), ())), preferred_element_type=F32)
        gf_v[rows, :] = g.astype(BF16)
        gf_copy(i).start()
        return 0

    lax.fori_loop(0, NCHUNK, gf_step, 0)
    loss_out[0] = jnp.sum(lg_v[1:2, :]) * (1.0 / ROWS)
    for s in range(LOCAL):
        pg_out[s] = (pg_v[s].astype(F32) * lg).astype(BF16)

    def gf_wait(i, _):
        gf_copy(i).wait()
        return 0

    lax.fori_loop(0, NCHUNK, gf_wait, 0)


def on_device(pooled, slot_of_table, partner, labels, w_first, b_first, w_head):
    vmem = pl.BlockSpec(memory_space=pltpu.VMEM)
    smem = pl.BlockSpec(memory_space=pltpu.SMEM)
    hbm = pl.BlockSpec(memory_space=pltpu.HBM)
    dma = pltpu.SemaphoreType.DMA
    tree = dma((len(TREE),))
    feat, act, a32, lg, sums = pl.pallas_call(
        kernel,
        out_shape=(
            jax.ShapeDtypeStruct((ROWS, FEAT), BF16),
            jax.ShapeDtypeStruct((ROWS, HID), F32),
            jax.ShapeDtypeStruct((ROWS, HID), F32),
            jax.ShapeDtypeStruct((8, ROWS), F32),
            jax.ShapeDtypeStruct((LOCAL, EMB, ROWS), BF16),
        ),
        in_specs=[hbm] * 7,
        out_specs=(vmem,) * 5,
        scratch_shapes=[
            pltpu.VMEM((FEAT, HID), BF16),
            pltpu.VMEM((ROWS, FEAT), BF16),
            pltpu.VMEM((SLOTS, RB, EMB), BF16),
            pltpu.VMEM((NC, RB, EMB), BF16),
            pltpu.VMEM((NC, RB, EMB), BF16),
            pltpu.VMEM((ROWS, HID), BF16),
            pltpu.VMEM((TAB, EMB, ROWS), BF16),
            pltpu.VMEM((NT, TAB, EB, ROWS), BF16),
            pltpu.VMEM((TAB + 1, EB, ROWS), BF16),
            pltpu.VMEM((SLOTS, EB, ROWS), BF16),
            pltpu.VMEM((1, ROWS), F32),
            pltpu.VMEM((NT, 1, ROWS), F32),
            pltpu.VMEM((1, ROWS), F32),
            pltpu.VMEM((NT, 1, ROWS), F32),
            pltpu.VMEM((1, ROWS), F32),
            pltpu.VMEM((NC, 1, ROWS), F32),
            pltpu.VMEM((1, HID), BF16),
            pltpu.VMEM((1, HID), BF16),
            pltpu.VMEM((1, ROWS), jnp.int32),
            pltpu.SMEM((TAB,), jnp.int32),
            pltpu.SMEM((NC,), jnp.int32),
            pltpu.VMEM((SLOTS, EMB), jnp.int32),
            pltpu.SMEM((SLOTS, EMB), jnp.int32),
            dma((6,)), dma,
            dma((NT,)), dma,
            tree, tree,
            dma((TAB,)), dma,
            dma((NC,)), dma,
            tree, tree,
            dma((NT,)), dma,
            dma((NT,)), dma,
            dma((NC,)), dma,
            dma((NT,)), dma,
            dma((NT,)), dma,
        ],
        compiler_params=pltpu.CompilerParams(
            collective_id=0, has_side_effects=True, vmem_limit_bytes=40 * 1024 * 1024
        ),
    )(
        slot_of_table, partner, labels.reshape(1, ROWS), jnp.transpose(pooled, (1, 0, 2)),
        w_first.reshape(FEAT, HID), b_first, w_head,
    )
    pg, gf, gb, gh, loss = pl.pallas_call(
        finish,
        out_shape=(
            jax.ShapeDtypeStruct((LOCAL, EMB, ROWS), BF16),
            jax.ShapeDtypeStruct((FEAT, HID), BF16),
            jax.ShapeDtypeStruct((1, HID), F32),
            jax.ShapeDtypeStruct((1, HID), F32),
            jax.ShapeDtypeStruct((1,), F32),
        ),
        in_specs=[vmem] * 5,
        out_specs=(vmem, hbm, vmem, vmem, smem),
        scratch_shapes=[
            pltpu.VMEM((ROWS, HID), BF16),
            pltpu.VMEM((FEAT, HID), BF16),
            dma((NCHUNK,)),
        ],
        compiler_params=pltpu.CompilerParams(vmem_limit_bytes=40 * 1024 * 1024),
    )(feat, act, a32, lg, sums)
    return pg, gf[None], gb, gh, loss


def solution(mesh):
    in_specs = (
        P("copy", "table", None), P(), P(), P("copy"), P("copy", None, "table"), P("copy", "table"), P("copy", "table"),
    )
    out_specs = (
        P("table", None, "copy"), P("copy", None, "table"), P("copy", "table"), P("copy", "table"), P("copy"),
    )
    return jax.shard_map(on_device, mesh=mesh, in_specs=in_specs, out_specs=out_specs, check_vma=False)
```

```python
import jax
import jax.numpy as jnp
from jax import lax
from jax.experimental import pallas as pl
from jax.experimental.pallas import tpu as pltpu
from jax.sharding import PartitionSpec as P

MESH = pl.DeviceIdType.MESH
F32, BF16 = jnp.float32, jnp.bfloat16
NT, NC = 8, 32
TAB, EMB, SLOTS, LOCAL = 26, 128, 40, 5
ROWS, HID, FEAT = 256, 512, 3328
RB = ROWS // NT
EB = EMB // NT
CH = 256
NCHUNK = FEAT // CH
HALF = FEAT // 2

A, B, BOTH = (0, RB // 2), (RB // 2, RB // 2), (0, RB)
ALL, LOW, HIGH = (0, FEAT), (0, HALF), (HALF, HALF)
TREE = (
    ((0, 0), (0, 1), A, ALL, "y"),
    ((0, 0), (0, 1), B, ALL, "y"),
    ((0, 0), (3, 0), BOTH, ALL, "right"),
    ((0, 0), (1, 0), BOTH, ALL, "left"),
    ((0, 1), (3, 1), A, ALL, "right"),
    ((0, 1), (1, 1), A, ALL, "left"),
    ((3, 0), (2, 0), BOTH, LOW, "right"),
    ((1, 0), (2, 0), BOTH, HIGH, "left"),
    ((3, 0), (3, 1), B, ALL, "y"),
    ((1, 0), (1, 1), B, ALL, "y"),
    ((3, 1), (2, 1), A, LOW, "right"),
    ((1, 1), (2, 1), A, HIGH, "left"),
    ((2, 0), (2, 1), B, ALL, "y"),
)
TREE_STEPS = (((), (0, 2, 3, 1)), ((0,), (4, 5)), ((2,), (6, 8)), ((3,), (7, 9)), ((4,), (10,)), ((5,), (11,)), ((6, 7), (12,)),
              ((1, 8, 9, 10, 11, 12), ()))


def relay_copy(t):
    return jnp.where(t < 24, (t // 3) * 4 + t % 3, jnp.where(t == 24, 3, 19))


def kernel(
    slot_h, partner_h, labels_h, pooled, w_hbm, b_h, h_h,
    gf_v, pg_out, gb_out, gh_out, loss_out,
    w_v, feat, feat_t, by_slot, relay_in, relay_out, act_v, a32_v, low_v, gt_v, in_b, in_a1, in_a2, in_low, in_high, in_al, in_ar,
    in_ay, in_l, in_r, sums, placed, pg_in,
    z_own, z_in, q_own, q_in, qs_own, qs_in, b_v, h_v, y_v, slot_s, partner_s, inv_v, inv_s,
    load_sem, inv_sem,
    a_send, a_recv, ag_send, ag_recv, c_send, c_recv, d_send, d_recv, tg_send, tg_recv,
    l_send, l_recv, m_send, m_recv, t_send, t_recv, r_send, r_recv, z_send, z_recv,
):
    c = lax.axis_index("copy")
    k = lax.axis_index("table")
    x, y = lax.rem(k, 4), k // 4
    my_rows = pl.ds(pl.multiple_of(k * RB, RB), RB)
    zq = lax.rem(c, 4)
    my_t = jnp.where(zq < 3, (c // 4) * 3 + zq, jnp.where(c == 3, 24, 25))
    is_relay = jnp.logical_or(zq < 3, jnp.logical_or(c == 3, c == 19))

    barrier = pltpu.get_barrier_semaphore()

    def greet_table(d, _):
        pl.semaphore_signal(barrier, inc=1, device_id=(c, lax.rem(k + d, NT)), device_id_type=MESH)
        return 0

    def greet_copy(d, _):
        pl.semaphore_signal(barrier, inc=1, device_id=(lax.rem(c + d, NC), k), device_id_type=MESH)
        return 0

    lax.fori_loop(1, NT, greet_table, 0)
    lax.fori_loop(1, NC, greet_copy, 0)

    loads = [
        pltpu.make_async_copy(src, dst, load_sem.at[i])
        for i, (src, dst) in enumerate(
            ((slot_h, slot_s), (partner_h, partner_s), (labels_h, y_v), (b_h, b_v), (h_h, h_v), (w_hbm, w_v))
        )
    ]
    for load in loads:
        load.start()
    pl.semaphore_wait(barrier, NT - 1 + NC - 1)

    def remote(src, dst, send, recv, copy, table):
        return pltpu.make_async_remote_copy(
            src_ref=src, dst_ref=dst, send_sem=send, recv_sem=recv, device_id=(copy, table), device_id_type=MESH
        )

    def over_table(fn):
        def body(d, _):
            fn(d, lax.rem(k + d, NT))
            return 0

        lax.fori_loop(1, NT, body, 0)

    def take(ref, sem):
        pltpu.make_async_copy(ref, ref, sem).wait()

    def share(step):
        return lax.rem(y + step[1], 2) * 4 + lax.rem(x + step[0], 4)

    target = {"y": share((0, 1)), "right": share((1, 0)), "left": share((3, 0))}

    def region(buf, origin, rows, cols):
        first = pl.multiple_of(share(origin) * RB + rows[0], RB // 2)
        return buf.at[pl.ds(first, rows[1]), pl.ds(cols[0], cols[1])]

    def tree_copy(buf, send, recv, i):
        origin, _, rows, cols, to = TREE[i]
        piece = region(buf, origin, rows, cols)
        return remote(piece, piece, send.at[i], recv.at[i], c, target[to])

    def tree_step(buf, send, recv, step):
        waits, starts = TREE_STEPS[step]
        for i in waits:
            _, origin, rows, cols, _ = TREE[i]
            take(region(buf, origin, rows, cols), recv.at[i])
        for i in starts:
            tree_copy(buf, send, recv, i).start()

    def a_copy(d, j):
        rows = pl.ds(pl.multiple_of(j * RB, RB), RB)
        return remote(pooled.at[:, rows, :], by_slot.at[pl.ds(k * LOCAL, LOCAL)], a_send.at[d], a_recv, c, j)

    over_table(lambda d, j: a_copy(d, j).start())
    pltpu.make_async_copy(pooled.at[:, my_rows, :], by_slot.at[pl.ds(k * LOCAL, LOCAL)], a_recv).start()
    for load in loads:
        load.wait()

    lane = lax.broadcasted_iota(jnp.int32, (8, EMB), 1)
    slots = jnp.full((8, EMB), SLOTS, jnp.int32)
    for t in range(TAB):
        slots = jnp.where(lane == t, slot_s[t], slots)
    for i in range(SLOTS // 8):
        found = jnp.where(lax.broadcasted_iota(jnp.int32, (8, EMB), 0) + 8 * i == slots, lane, TAB)
        inv_v[8 * i : 8 * i + 8, :] = jnp.broadcast_to(jnp.min(found, axis=1, keepdims=True), (8, EMB))
    inv_copy = pltpu.make_async_copy(inv_v, inv_s, inv_sem)
    inv_copy.start()

    take(by_slot, a_recv)
    for t in range(TAB):
        feat[my_rows, t * EMB : (t + 1) * EMB] = by_slot[slot_s[t]]

    tree_step(feat, ag_send, ag_recv, 0)

    def c_copy(i):
        t = lax.rem(i + my_t, TAB)
        to = relay_copy(t)
        src = feat.at[my_rows, pl.ds(pl.multiple_of(t * EMB, EMB), EMB)]
        return src, to, remote(src, relay_in.at[c], c_send.at[i], c_recv, to, k)

    def c_start(i, _):
        src, to, copy = c_copy(i)

        @pl.when(to != c)
        def _():
            copy.start()

        @pl.when(to == c)
        def _():
            pltpu.make_async_copy(src, relay_in.at[c], c_recv).start()

        return 0

    lax.fori_loop(0, TAB, c_start, 0)
    for step in range(1, 6):
        tree_step(feat, ag_send, ag_recv, step)

    my_cols = pl.ds(pl.multiple_of(my_t * EMB, EMB), EMB)

    def d_copy(d, p):
        return remote(relay_out.at[p], feat_t.at[my_rows, my_cols], d_send.at[d], d_recv, p, k)

    @pl.when(is_relay)
    def _():
        take(relay_in, c_recv)

        def pick(p, _):
            relay_out[p] = relay_in[partner_s[p]]
            return 0

        lax.fori_loop(0, NC, pick, 0, unroll=4)

        def d_start(d, _):
            d_copy(d, lax.rem(c + d, NC)).start()
            return 0

        lax.fori_loop(1, NC, d_start, 0)
        pltpu.make_async_copy(relay_out.at[c], feat_t.at[my_rows, my_cols], d_recv).start()

    for step in range(6, len(TREE_STEPS)):
        tree_step(feat, ag_send, ag_recv, step)

    def head_row(total):
        return jnp.sum(jnp.transpose(total), axis=0, keepdims=True)

    total = jnp.zeros((ROWS, EMB), F32)
    for n in range(HID // CH):
        cols = slice(n * CH, (n + 1) * CH)
        head = h_v[:, cols].astype(F32)
        pre = jnp.dot(feat[...], w_v[:, cols], preferred_element_type=F32) + b_v[:, cols].astype(F32)
        sig = jax.nn.sigmoid(pre)
        act = pre * sig
        act_v[:, cols] = act
        a32 = head * (sig * (1.0 + pre * (1.0 - sig)))
        a32_v[:, cols] = a32
        low_v[:, cols] = a32.astype(BF16)
        weighed = act * head
        total = total + (weighed[:, :EMB] + weighed[:, EMB:])
    z_own[...] = head_row(total)

    z_in[k] = z_own[...]

    def l_copy(d, j):
        return remote(z_own, z_in.at[k], l_send.at[d], l_recv, c, j)

    over_table(lambda d, j: l_copy(d, j).start())

    take(feat_t.at[my_rows], d_recv)
    tree_step(feat_t, tg_send, tg_recv, 0)

    def gt_step(i, _):
        rows = pl.ds(pl.multiple_of(i * CH, CH), CH)
        g = lax.dot_general(w_v[rows, :], low_v[...], (((1,), (1,)), ((), ())), preferred_element_type=F32)
        gt_v[pl.ds(i * 2, 2)] = g.astype(BF16).reshape(2, EMB, ROWS)
        return 0

    lax.fori_loop(0, NCHUNK, gt_step, 0)

    for step in range(1, 7):
        tree_step(feat_t, tg_send, tg_recv, step)

    def part(step, tables=(0, TAB), lanes=(0, ROWS)):
        first = pl.multiple_of(share(step) * EB, EB)
        return pl.ds(tables[0], tables[1]), pl.ds(first, EB), pl.ds(lanes[0], lanes[1])

    ta, tb = (0, TAB // 2), (TAB // 2, TAB // 2)
    low, high = (0, EMB), (EMB, EMB)
    sends = []

    def reduce_send(step, tables, lanes, dst, to):
        i = len(sends)
        where = part(step, tables, lanes)
        copy = remote(gt_v.at[where], dst, r_send.at[i], r_recv.at[i], c, target[to])
        copy.start()
        sends.append(copy)

    def add(step, tables, lanes, *arrived):
        where = part(step, tables, lanes)
        total = gt_v[where].astype(F32)
        for ref, i in arrived:
            take(ref, r_recv.at[i])
            total = total + ref[...].astype(F32)
        gt_v[where] = total.astype(BF16)

    full = (0, ROWS)
    every = (0, TAB)
    reduce_send((2, 1), tb, full, in_b.at[0], "y")
    reduce_send((2, 1), ta, low, in_a1, "left")
    reduce_send((2, 1), ta, high, in_a2, "right")
    reduce_send((3, 1), tb, full, in_b.at[1], "y")
    reduce_send((1, 1), tb, full, in_b.at[2], "y")
    reduce_send((0, 1), tb, full, in_b.at[3], "y")

    tree_step(feat_t, tg_send, tg_recv, 7)
    total = jnp.zeros((ROWS, EMB), F32)
    for n in range(HID // CH):
        cols = slice(n * CH, (n + 1) * CH)
        pre = jnp.dot(feat_t[...], w_v[:, cols], preferred_element_type=F32) + b_v[:, cols].astype(F32)
        weighed = pre * jax.nn.sigmoid(pre) * h_v[:, cols].astype(F32)
        total = total + (weighed[:, :EMB] + weighed[:, EMB:])
    q_own[...] = head_row(total)
    q_in[k] = q_own[...]

    def m_copy(d, j):
        return remote(q_own, q_in.at[k], m_send.at[d], m_recv, c, j)

    over_table(lambda d, j: m_copy(d, j).start())

    add((2, 0), tb, full, (in_b.at[0], 0))
    reduce_send((2, 0), every, low, in_low, "left")
    reduce_send((2, 0), every, high, in_high, "right")
    add((3, 1), ta, low, (in_a1, 1))
    reduce_send((3, 1), ta, full, in_al, "left")
    add((1, 1), ta, high, (in_a2, 2))
    reduce_send((1, 1), ta, full, in_ar, "right")

    take(z_in.at[pl.ds(0, NT - 1)], l_recv)
    take(q_in.at[pl.ds(0, NT - 1)], m_recv)
    qs_own[...] = jnp.sum(q_in[...], axis=0)
    qs_in[c] = qs_own[...]

    def t_copy(d):
        return remote(qs_own, qs_in.at[c], t_send.at[d], t_recv, lax.rem(c + d, NC), k)

    def t_start(d, _):
        t_copy(d).start()
        return 0

    lax.fori_loop(1, NC, t_start, 0)

    add((3, 0), tb, full, (in_b.at[1], 3))
    add((3, 0), every, low, (in_low, 6))
    reduce_send((3, 0), every, full, in_l, "left")
    add((1, 0), tb, full, (in_b.at[2], 4))
    add((1, 0), every, high, (in_high, 7))
    reduce_send((1, 0), every, full, in_r, "right")
    add((0, 1), ta, full, (in_al, 8), (in_ar, 9))
    reduce_send((0, 1), ta, full, in_ay, "y")

    take(qs_in.at[pl.ds(0, NC - 1)], t_recv)
    z = jnp.sum(z_in[...], axis=0)
    q = jax.nn.sigmoid(qs_in[partner_s[c]])
    target_y = y_v[...].astype(F32)
    soft = jnp.maximum(z, 0.0) + jnp.log1p(jnp.exp(-jnp.abs(z)))
    lg = 2.0 * jax.nn.sigmoid(z) - target_y - q
    loss_out[...] = jnp.broadcast_to(
        jnp.sum(2.0 * soft - target_y * z - q * z, axis=1, keepdims=True) * (1.0 / ROWS), (1, EMB)
    )
    lg_col = jnp.transpose(jnp.broadcast_to(lg, (EMB, ROWS)))
    for n in range(HID // EMB):
        cols = slice(n * EMB, (n + 1) * EMB)
        grad_pre = lg_col * a32_v[:, cols]
        low_v[:, cols] = grad_pre.astype(BF16)
        gb_out[:, cols] = jnp.sum(grad_pre, axis=0, keepdims=True)
        gh_out[:, cols] = jnp.sum(lg_col * act_v[:, cols], axis=0, keepdims=True)

    for ref, i in ((in_b.at[3], 5), (in_l, 10), (in_r, 11), (in_ay, 12)):
        take(ref, r_recv.at[i])
    inv_copy.wait()
    mine = pl.ds(pl.multiple_of(k * EB, EB), EB)
    half = TAB // 2
    total = gt_v[0:half, mine, :].astype(F32) + in_ay[...].astype(F32)
    total = total + in_l[0:half].astype(F32) + in_r[0:half].astype(F32)
    sums[0:half] = (total * lg[None]).astype(BF16)
    total = gt_v[half:TAB, mine, :].astype(F32) + in_b[3].astype(F32)
    total = total + in_l[half:TAB].astype(F32) + in_r[half:TAB].astype(F32)
    sums[half:TAB] = (total * lg[None]).astype(BF16)
    sums[TAB] = jnp.zeros((EB, ROWS), BF16)

    def place(s, _):
        placed[s] = sums[inv_s[s, 0]]
        return 0

    lax.fori_loop(0, SLOTS, place, 0, unroll=4)

    def z_copy(d, j):
        return remote(placed.at[pl.ds(j * LOCAL, LOCAL)], pg_in.at[:, mine, :], z_send.at[d], z_recv, c, j)

    over_table(lambda d, j: z_copy(d, j).start())
    pltpu.make_async_copy(placed.at[pl.ds(k * LOCAL, LOCAL)], pg_in.at[:, mine, :], z_recv).start()

    def gf_step(i, _):
        rows = pl.ds(pl.multiple_of(i * CH, CH), CH)
        g = lax.dot_general(feat[:, rows], low_v[...], (((0,), (0,)), ((), ())), preferred_element_type=F32)
        gf_v[rows, :] = g.astype(BF16)
        return 0

    lax.fori_loop(0, NCHUNK, gf_step, 0)

    over_table(lambda d, j: a_copy(d, j).wait_send())

    def c_wait(i, _):
        _, to, copy = c_copy(i)

        @pl.when(to != c)
        def _():
            copy.wait_send()

        return 0

    lax.fori_loop(0, TAB, c_wait, 0)
    for i in range(len(TREE)):
        tree_copy(feat, ag_send, ag_recv, i).wait_send()
        tree_copy(feat_t, tg_send, tg_recv, i).wait_send()

    @pl.when(is_relay)
    def _():
        def d_wait(d, _):
            d_copy(d, lax.rem(c + d, NC)).wait_send()
            return 0

        lax.fori_loop(1, NC, d_wait, 0)

    def t_wait(d, _):
        t_copy(d).wait_send()
        return 0

    lax.fori_loop(1, NC, t_wait, 0)

    def rest(d, j):
        l_copy(d, j).wait_send()
        m_copy(d, j).wait_send()
        z_copy(d, j).wait_send()

    over_table(rest)
    for copy in sends:
        copy.wait_send()
    take(pg_in, z_recv)
    pg_out[...] = pg_in[...]


def finish(gf_v, pg_v, gb_v, gh_v, loss_v, pg_out, gf_out, gb_out, gh_out, loss_out, sem):
    copies = [pltpu.make_async_copy(gf_v, gf_out, sem.at[0]), pltpu.make_async_copy(pg_v, pg_out, sem.at[1])]
    for copy in copies:
        copy.start()
    gb_out[...] = gb_v[...]
    gh_out[...] = gh_v[...]
    loss_out[0] = jnp.sum(loss_v[:, 0:1])
    for copy in copies:
        copy.wait()


def on_device(pooled, slot_of_table, partner, labels, w_first, b_first, w_head):
    vmem = pl.BlockSpec(memory_space=pltpu.VMEM)
    smem = pl.BlockSpec(memory_space=pltpu.SMEM)
    hbm = pl.BlockSpec(memory_space=pltpu.HBM)
    dma = pltpu.SemaphoreType.DMA
    tree = dma((len(TREE),))
    results = pl.pallas_call(
        kernel,
        out_shape=(
            jax.ShapeDtypeStruct((FEAT, HID), BF16),
            jax.ShapeDtypeStruct((LOCAL, EMB, ROWS), BF16),
            jax.ShapeDtypeStruct((1, HID), F32),
            jax.ShapeDtypeStruct((1, HID), F32),
            jax.ShapeDtypeStruct((1, EMB), F32),
        ),
        in_specs=[hbm] * 7,
        out_specs=(vmem,) * 5,
        scratch_shapes=[
            pltpu.VMEM((FEAT, HID), BF16),
            pltpu.VMEM((ROWS, FEAT), BF16),
            pltpu.VMEM((ROWS, FEAT), BF16),
            pltpu.VMEM((SLOTS, RB, EMB), BF16),
            pltpu.VMEM((NC, RB, EMB), BF16),
            pltpu.VMEM((NC, RB, EMB), BF16),
            pltpu.VMEM((ROWS, HID), F32),
            pltpu.VMEM((ROWS, HID), F32),
            pltpu.VMEM((ROWS, HID), BF16),
            pltpu.VMEM((TAB, EMB, ROWS), BF16),
            pltpu.VMEM((4, TAB // 2, EB, ROWS), BF16),
            pltpu.VMEM((TAB // 2, EB, EMB), BF16),
            pltpu.VMEM((TAB // 2, EB, EMB), BF16),
            pltpu.VMEM((TAB, EB, EMB), BF16),
            pltpu.VMEM((TAB, EB, EMB), BF16),
            pltpu.VMEM((TAB // 2, EB, ROWS), BF16),
            pltpu.VMEM((TAB // 2, EB, ROWS), BF16),
            pltpu.VMEM((TAB // 2, EB, ROWS), BF16),
            pltpu.VMEM((TAB, EB, ROWS), BF16),
            pltpu.VMEM((TAB, EB, ROWS), BF16),
            pltpu.VMEM((TAB + 1, EB, ROWS), BF16),
            pltpu.VMEM((SLOTS, EB, ROWS), BF16),
            pltpu.VMEM((LOCAL, EMB, ROWS), BF16),
            pltpu.VMEM((1, ROWS), F32),
            pltpu.VMEM((NT, 1, ROWS), F32),
            pltpu.VMEM((1, ROWS), F32),
            pltpu.VMEM((NT, 1, ROWS), F32),
            pltpu.VMEM((1, ROWS), F32),
            pltpu.VMEM((NC, 1, ROWS), F32),
            pltpu.VMEM((1, HID), BF16),
            pltpu.VMEM((1, HID), BF16),
            pltpu.VMEM((1, ROWS), jnp.int32),
            pltpu.SMEM((TAB,), jnp.int32),
            pltpu.SMEM((NC,), jnp.int32),
            pltpu.VMEM((SLOTS, EMB), jnp.int32),
            pltpu.SMEM((SLOTS, EMB), jnp.int32),
            dma((6,)), dma,
            dma((NT,)), dma,
            tree, tree,
            dma((TAB,)), dma,
            dma((NC,)), dma,
            tree, tree,
            dma((NT,)), dma,
            dma((NT,)), dma,
            dma((NC,)), dma,
            tree, tree,
            dma((NT,)), dma,
        ],
        compiler_params=pltpu.CompilerParams(
            collective_id=0, has_side_effects=True, vmem_limit_bytes=40 * 1024 * 1024
        ),
    )(
        *(
            pltpu.with_memory_space_constraint(v, pltpu.HBM)
            for v in (
                slot_of_table, partner, labels.reshape(1, ROWS), jnp.transpose(pooled, (1, 0, 2)),
                w_first.reshape(FEAT, HID), b_first, w_head,
            )
        )
    )
    pg, gf, gb, gh, loss = pl.pallas_call(
        finish,
        out_shape=(
            jax.ShapeDtypeStruct((LOCAL, EMB, ROWS), BF16),
            jax.ShapeDtypeStruct((FEAT, HID), BF16),
            jax.ShapeDtypeStruct((1, HID), F32),
            jax.ShapeDtypeStruct((1, HID), F32),
            jax.ShapeDtypeStruct((1,), F32),
        ),
        in_specs=[vmem] * 5,
        out_specs=(hbm, hbm, vmem, vmem, smem),
        scratch_shapes=[dma((2,))],
        compiler_params=pltpu.CompilerParams(vmem_limit_bytes=24 * 1024 * 1024),
    )(*results)
    return pg, gf[None], gb, gh, loss


def solution(mesh):
    in_specs = (
        P("copy", "table", None), P(), P(), P("copy"), P("copy", None, "table"), P("copy", "table"), P("copy", "table"),
    )
    out_specs = (
        P("table", None, "copy"), P("copy", None, "table"), P("copy", "table"), P("copy", "table"), P("copy"),
    )
    return jax.shard_map(on_device, mesh=mesh, in_specs=in_specs, out_specs=out_specs, check_vma=False)
```

```python
import jax
import jax.numpy as jnp
from jax import lax
from jax.experimental import pallas as pl
from jax.experimental.pallas import tpu as pltpu
from jax.sharding import PartitionSpec as P

MESH = pl.DeviceIdType.MESH
F32, BF16 = jnp.float32, jnp.bfloat16
NT, NC = 8, 32
TAB, EMB, SLOTS, LOCAL = 26, 128, 40, 5
ROWS, HID, FEAT = 256, 512, 3328
RB = ROWS // NT
EB = EMB // NT
CH = 256
NCHUNK = FEAT // CH
HALF = FEAT // 2

A, B, BOTH = (0, RB // 2), (RB // 2, RB // 2), (0, RB)
ALL, LOW, HIGH = (0, FEAT), (0, HALF), (HALF, HALF)
TREE = (
    ((0, 0), (0, 1), A, ALL, "y"),
    ((0, 0), (0, 1), B, ALL, "y"),
    ((0, 0), (3, 0), BOTH, ALL, "right"),
    ((0, 0), (1, 0), BOTH, ALL, "left"),
    ((0, 1), (3, 1), A, ALL, "right"),
    ((0, 1), (1, 1), A, ALL, "left"),
    ((3, 0), (2, 0), BOTH, LOW, "right"),
    ((1, 0), (2, 0), BOTH, HIGH, "left"),
    ((3, 0), (3, 1), B, ALL, "y"),
    ((1, 0), (1, 1), B, ALL, "y"),
    ((3, 1), (2, 1), A, LOW, "right"),
    ((1, 1), (2, 1), A, HIGH, "left"),
    ((2, 0), (2, 1), B, ALL, "y"),
)
TREE_STEPS = (((), (0, 2, 3, 1)), ((0,), (4, 5)), ((2,), (6, 8)), ((3,), (7, 9)), ((4,), (10,)), ((5,), (11,)), ((6, 7), (12,)),
              ((1, 8, 9, 10, 11, 12), ()))


def relay_copy(t):
    return jnp.where(t < 24, (t // 3) * 4 + t % 3, jnp.where(t == 24, 3, 19))


def kernel(
    slot_h, partner_h, labels_h, pooled, w_hbm, b_h, h_h,
    gf_v, pg_out, gb_out, gh_out, loss_out,
    w_v, feat, feat_t, by_slot, relay_in, relay_out, act_v, a32_v, low_v, gt_v, in_b, in_a1, in_a2, in_low, in_high, in_al, in_ar,
    in_ay, in_l, in_r, sums, placed, pg_in,
    z_own, z_in, q_own, q_in, qs_own, qs_in, b_v, h_v, y_v, slot_s, partner_s, inv_v, inv_s,
    in_sem, go_sem, load_sem, inv_sem,
    a_send, a_recv, ag_send, ag_recv, c_send, c_recv, d_send, d_recv, tg_send, tg_recv,
    l_send, l_recv, m_send, m_recv, t_send, t_recv, r_send, r_recv, z_send, z_recv,
):
    c = lax.axis_index("copy")
    k = lax.axis_index("table")
    x, y = lax.rem(k, 4), k // 4
    my_rows = pl.ds(pl.multiple_of(k * RB, RB), RB)
    zq = lax.rem(c, 4)
    my_t = jnp.where(zq < 3, (c // 4) * 3 + zq, jnp.where(c == 3, 24, 25))
    is_relay = jnp.logical_or(zq < 3, jnp.logical_or(c == 3, c == 19))

    barrier = pltpu.get_barrier_semaphore()

    is_gate = k == 0

    def signal(sem, copy, table):
        pl.semaphore_signal(sem, inc=1, device_id=(copy, table), device_id_type=MESH)

    def greet_table(d, _):
        j = lax.rem(k + d, NT)

        @pl.when(j != 0)
        def _():
            signal(barrier, c, j)

        return 0

    lax.fori_loop(1, NT, greet_table, 0)

    loads = [
        pltpu.make_async_copy(src, dst, load_sem.at[i])
        for i, (src, dst) in enumerate(
            ((slot_h, slot_s), (partner_h, partner_s), (labels_h, y_v), (b_h, b_v), (h_h, h_v), (w_hbm, w_v))
        )
    ]
    for load in loads:
        load.start()

    @pl.when(jnp.logical_not(is_gate))
    def _():
        pl.semaphore_wait(barrier, NT - 1)
        signal(in_sem, c, 0)

    @pl.when(is_gate)
    def _():
        pl.semaphore_wait(in_sem, NT - 1)

        def greet_copy(d, _):
            signal(barrier, lax.rem(c + d, NC), k)
            return 0

        lax.fori_loop(1, NC, greet_copy, 0)

    def all_in():
        @pl.when(is_gate)
        def _():
            pl.semaphore_wait(barrier, NC - 1)
            for j in range(1, NT):
                signal(go_sem, c, j)

        @pl.when(jnp.logical_not(is_gate))
        def _():
            pl.semaphore_wait(go_sem, 1)

    def remote(src, dst, send, recv, copy, table):
        return pltpu.make_async_remote_copy(
            src_ref=src, dst_ref=dst, send_sem=send, recv_sem=recv, device_id=(copy, table), device_id_type=MESH
        )

    def over_table(fn):
        def body(d, _):
            fn(d, lax.rem(k + d, NT))
            return 0

        lax.fori_loop(1, NT, body, 0)

    def take(ref, sem):
        pltpu.make_async_copy(ref, ref, sem).wait()

    def share(step):
        return lax.rem(y + step[1], 2) * 4 + lax.rem(x + step[0], 4)

    target = {"y": share((0, 1)), "right": share((1, 0)), "left": share((3, 0))}

    def region(buf, origin, rows, cols):
        first = pl.multiple_of(share(origin) * RB + rows[0], RB // 2)
        return buf.at[pl.ds(first, rows[1]), pl.ds(cols[0], cols[1])]

    def tree_copy(buf, send, recv, i):
        origin, _, rows, cols, to = TREE[i]
        piece = region(buf, origin, rows, cols)
        return remote(piece, piece, send.at[i], recv.at[i], c, target[to])

    def tree_step(buf, send, recv, step):
        waits, starts = TREE_STEPS[step]
        for i in waits:
            _, origin, rows, cols, _ = TREE[i]
            take(region(buf, origin, rows, cols), recv.at[i])
        for i in starts:
            tree_copy(buf, send, recv, i).start()

    def a_copy(d, j):
        rows = pl.ds(pl.multiple_of(j * RB, RB), RB)
        return remote(pooled.at[:, rows, :], by_slot.at[pl.ds(k * LOCAL, LOCAL)], a_send.at[d], a_recv, c, j)

    over_table(lambda d, j: a_copy(d, j).start())
    pltpu.make_async_copy(pooled.at[:, my_rows, :], by_slot.at[pl.ds(k * LOCAL, LOCAL)], a_recv).start()
    for load in loads:
        load.wait()

    lane = lax.broadcasted_iota(jnp.int32, (8, EMB), 1)
    slots = jnp.full((8, EMB), SLOTS, jnp.int32)
    for t in range(TAB):
        slots = jnp.where(lane == t, slot_s[t], slots)
    for i in range(SLOTS // 8):
        found = jnp.where(lax.broadcasted_iota(jnp.int32, (8, EMB), 0) + 8 * i == slots, lane, TAB)
        inv_v[8 * i : 8 * i + 8, :] = jnp.broadcast_to(jnp.min(found, axis=1, keepdims=True), (8, EMB))
    inv_copy = pltpu.make_async_copy(inv_v, inv_s, inv_sem)
    inv_copy.start()

    take(by_slot, a_recv)
    for t in range(TAB):
        feat[my_rows, t * EMB : (t + 1) * EMB] = by_slot[slot_s[t]]

    tree_step(feat, ag_send, ag_recv, 0)

    def c_copy(i):
        t = lax.rem(i + my_t, TAB)
        to = relay_copy(t)
        src = feat.at[my_rows, pl.ds(pl.multiple_of(t * EMB, EMB), EMB)]
        return src, to, remote(src, relay_in.at[c], c_send.at[i], c_recv, to, k)

    def c_start(i, _):
        src, to, copy = c_copy(i)

        @pl.when(to != c)
        def _():
            copy.start()

        @pl.when(to == c)
        def _():
            pltpu.make_async_copy(src, relay_in.at[c], c_recv).start()

        return 0

    all_in()
    lax.fori_loop(0, TAB, c_start, 0)
    for step in range(1, 6):
        tree_step(feat, ag_send, ag_recv, step)

    my_cols = pl.ds(pl.multiple_of(my_t * EMB, EMB), EMB)

    def d_copy(d, p):
        return remote(relay_out.at[p], feat_t.at[my_rows, my_cols], d_send.at[d], d_recv, p, k)

    @pl.when(is_relay)
    def _():
        take(relay_in, c_recv)

        def pick(p, _):
            relay_out[p] = relay_in[partner_s[p]]
            return 0

        lax.fori_loop(0, NC, pick, 0, unroll=4)

        def d_start(d, _):
            d_copy(d, lax.rem(c + d, NC)).start()
            return 0

        lax.fori_loop(1, NC, d_start, 0)
        pltpu.make_async_copy(relay_out.at[c], feat_t.at[my_rows, my_cols], d_recv).start()

    for step in range(6, len(TREE_STEPS)):
        tree_step(feat, ag_send, ag_recv, step)

    def head_row(total):
        return jnp.sum(jnp.transpose(total), axis=0, keepdims=True)

    total = jnp.zeros((ROWS, EMB), F32)
    for n in range(HID // CH):
        cols = slice(n * CH, (n + 1) * CH)
        head = h_v[:, cols].astype(F32)
        pre = jnp.dot(feat[...], w_v[:, cols], preferred_element_type=F32) + b_v[:, cols].astype(F32)
        sig = jax.nn.sigmoid(pre)
        act = pre * sig
        act_v[:, cols] = act
        a32 = head * (sig * (1.0 + pre * (1.0 - sig)))
        a32_v[:, cols] = a32
        low_v[:, cols] = a32.astype(BF16)
        weighed = act * head
        total = total + (weighed[:, :EMB] + weighed[:, EMB:])
    z_own[...] = head_row(total)

    z_in[k] = z_own[...]

    def l_copy(d, j):
        return remote(z_own, z_in.at[k], l_send.at[d], l_recv, c, j)

    over_table(lambda d, j: l_copy(d, j).start())

    take(feat_t.at[my_rows], d_recv)
    tree_step(feat_t, tg_send, tg_recv, 0)

    def gt_step(i, _):
        rows = pl.ds(pl.multiple_of(i * CH, CH), CH)
        g = lax.dot_general(w_v[rows, :], low_v[...], (((1,), (1,)), ((), ())), preferred_element_type=F32)
        gt_v[pl.ds(i * 2, 2)] = g.astype(BF16).reshape(2, EMB, ROWS)
        return 0

    lax.fori_loop(0, NCHUNK, gt_step, 0)

    for step in range(1, 7):
        tree_step(feat_t, tg_send, tg_recv, step)

    def part(step, tables=(0, TAB), lanes=(0, ROWS)):
        first = pl.multiple_of(share(step) * EB, EB)
        return pl.ds(tables[0], tables[1]), pl.ds(first, EB), pl.ds(lanes[0], lanes[1])

    ta, tb = (0, TAB // 2), (TAB // 2, TAB // 2)
    low, high = (0, EMB), (EMB, EMB)
    sends = []

    def reduce_send(step, tables, lanes, dst, to):
        i = len(sends)
        where = part(step, tables, lanes)
        copy = remote(gt_v.at[where], dst, r_send.at[i], r_recv.at[i], c, target[to])
        copy.start()
        sends.append(copy)

    def add(step, tables, lanes, *arrived):
        where = part(step, tables, lanes)
        total = gt_v[where].astype(F32)
        for ref, i in arrived:
            take(ref, r_recv.at[i])
            total = total + ref[...].astype(F32)
        gt_v[where] = total.astype(BF16)

    full = (0, ROWS)
    every = (0, TAB)
    reduce_send((2, 1), tb, full, in_b.at[0], "y")
    reduce_send((2, 1), ta, low, in_a1, "left")
    reduce_send((2, 1), ta, high, in_a2, "right")
    reduce_send((3, 1), tb, full, in_b.at[1], "y")
    reduce_send((1, 1), tb, full, in_b.at[2], "y")
    reduce_send((0, 1), tb, full, in_b.at[3], "y")

    tree_step(feat_t, tg_send, tg_recv, 7)
    total = jnp.zeros((ROWS, EMB), F32)
    for n in range(HID // CH):
        cols = slice(n * CH, (n + 1) * CH)
        pre = jnp.dot(feat_t[...], w_v[:, cols], preferred_element_type=F32) + b_v[:, cols].astype(F32)
        weighed = pre * jax.nn.sigmoid(pre) * h_v[:, cols].astype(F32)
        total = total + (weighed[:, :EMB] + weighed[:, EMB:])
    q_own[...] = head_row(total)
    q_in[k] = q_own[...]

    def m_copy(d, j):
        return remote(q_own, q_in.at[k], m_send.at[d], m_recv, c, j)

    over_table(lambda d, j: m_copy(d, j).start())

    add((2, 0), tb, full, (in_b.at[0], 0))
    reduce_send((2, 0), every, low, in_low, "left")
    reduce_send((2, 0), every, high, in_high, "right")
    add((3, 1), ta, low, (in_a1, 1))
    reduce_send((3, 1), ta, full, in_al, "left")
    add((1, 1), ta, high, (in_a2, 2))
    reduce_send((1, 1), ta, full, in_ar, "right")

    take(z_in.at[pl.ds(0, NT - 1)], l_recv)
    take(q_in.at[pl.ds(0, NT - 1)], m_recv)
    qs_own[...] = jnp.sum(q_in[...], axis=0)
    qs_in[c] = qs_own[...]

    def t_copy(d):
        return remote(qs_own, qs_in.at[c], t_send.at[d], t_recv, lax.rem(c + d, NC), k)

    def t_start(d, _):
        t_copy(d).start()
        return 0

    lax.fori_loop(1, NC, t_start, 0)

    add((3, 0), tb, full, (in_b.at[1], 3))
    add((3, 0), every, low, (in_low, 6))
    reduce_send((3, 0), every, full, in_l, "left")
    add((1, 0), tb, full, (in_b.at[2], 4))
    add((1, 0), every, high, (in_high, 7))
    reduce_send((1, 0), every, full, in_r, "right")
    add((0, 1), ta, full, (in_al, 8), (in_ar, 9))
    reduce_send((0, 1), ta, full, in_ay, "y")

    take(qs_in.at[pl.ds(0, NC - 1)], t_recv)
    z = jnp.sum(z_in[...], axis=0)
    q = jax.nn.sigmoid(qs_in[partner_s[c]])
    target_y = y_v[...].astype(F32)
    soft = jnp.maximum(z, 0.0) + jnp.log1p(jnp.exp(-jnp.abs(z)))
    lg = 2.0 * jax.nn.sigmoid(z) - target_y - q
    loss_out[...] = jnp.broadcast_to(
        jnp.sum(2.0 * soft - target_y * z - q * z, axis=1, keepdims=True) * (1.0 / ROWS), (1, EMB)
    )
    lg_col = jnp.transpose(jnp.broadcast_to(lg, (EMB, ROWS)))
    for n in range(HID // EMB):
        cols = slice(n * EMB, (n + 1) * EMB)
        grad_pre = lg_col * a32_v[:, cols]
        low_v[:, cols] = grad_pre.astype(BF16)
        gb_out[:, cols] = jnp.sum(grad_pre, axis=0, keepdims=True)
        gh_out[:, cols] = jnp.sum(lg_col * act_v[:, cols], axis=0, keepdims=True)

    for ref, i in ((in_b.at[3], 5), (in_l, 10), (in_r, 11), (in_ay, 12)):
        take(ref, r_recv.at[i])
    inv_copy.wait()
    mine = pl.ds(pl.multiple_of(k * EB, EB), EB)
    half = TAB // 2
    total = gt_v[0:half, mine, :].astype(F32) + in_ay[...].astype(F32)
    total = total + in_l[0:half].astype(F32) + in_r[0:half].astype(F32)
    sums[0:half] = (total * lg[None]).astype(BF16)
    total = gt_v[half:TAB, mine, :].astype(F32) + in_b[3].astype(F32)
    total = total + in_l[half:TAB].astype(F32) + in_r[half:TAB].astype(F32)
    sums[half:TAB] = (total * lg[None]).astype(BF16)
    sums[TAB] = jnp.zeros((EB, ROWS), BF16)

    def place(s, _):
        placed[s] = sums[inv_s[s, 0]]
        return 0

    lax.fori_loop(0, SLOTS, place, 0, unroll=4)

    def z_copy(d, j):
        return remote(placed.at[pl.ds(j * LOCAL, LOCAL)], pg_in.at[:, mine, :], z_send.at[d], z_recv, c, j)

    over_table(lambda d, j: z_copy(d, j).start())
    pltpu.make_async_copy(placed.at[pl.ds(k * LOCAL, LOCAL)], pg_in.at[:, mine, :], z_recv).start()

    def gf_step(i, _):
        rows = pl.ds(pl.multiple_of(i * CH, CH), CH)
        g = lax.dot_general(feat[:, rows], low_v[...], (((0,), (0,)), ((), ())), preferred_element_type=F32)
        gf_v[rows, :] = g.astype(BF16)
        return 0

    lax.fori_loop(0, NCHUNK, gf_step, 0)

    over_table(lambda d, j: a_copy(d, j).wait_send())

    def c_wait(i, _):
        _, to, copy = c_copy(i)

        @pl.when(to != c)
        def _():
            copy.wait_send()

        return 0

    lax.fori_loop(0, TAB, c_wait, 0)
    for i in range(len(TREE)):
        tree_copy(feat, ag_send, ag_recv, i).wait_send()
        tree_copy(feat_t, tg_send, tg_recv, i).wait_send()

    @pl.when(is_relay)
    def _():
        def d_wait(d, _):
            d_copy(d, lax.rem(c + d, NC)).wait_send()
            return 0

        lax.fori_loop(1, NC, d_wait, 0)

    def t_wait(d, _):
        t_copy(d).wait_send()
        return 0

    lax.fori_loop(1, NC, t_wait, 0)

    def rest(d, j):
        l_copy(d, j).wait_send()
        m_copy(d, j).wait_send()
        z_copy(d, j).wait_send()

    over_table(rest)
    for copy in sends:
        copy.wait_send()
    take(pg_in, z_recv)
    pg_out[...] = pg_in[...]


def finish(gf_v, pg_v, gb_v, gh_v, loss_v, pg_out, gf_out, gb_out, gh_out, loss_out, sem):
    copies = [pltpu.make_async_copy(gf_v, gf_out, sem.at[0]), pltpu.make_async_copy(pg_v, pg_out, sem.at[1])]
    for copy in copies:
        copy.start()
    gb_out[...] = gb_v[...]
    gh_out[...] = gh_v[...]
    loss_out[0] = jnp.sum(loss_v[:, 0:1])
    for copy in copies:
        copy.wait()


def on_device(pooled, slot_of_table, partner, labels, w_first, b_first, w_head):
    vmem = pl.BlockSpec(memory_space=pltpu.VMEM)
    smem = pl.BlockSpec(memory_space=pltpu.SMEM)
    hbm = pl.BlockSpec(memory_space=pltpu.HBM)
    dma = pltpu.SemaphoreType.DMA
    tree = dma((len(TREE),))
    results = pl.pallas_call(
        kernel,
        out_shape=(
            jax.ShapeDtypeStruct((FEAT, HID), BF16),
            jax.ShapeDtypeStruct((LOCAL, EMB, ROWS), BF16),
            jax.ShapeDtypeStruct((1, HID), F32),
            jax.ShapeDtypeStruct((1, HID), F32),
            jax.ShapeDtypeStruct((1, EMB), F32),
        ),
        in_specs=[hbm] * 7,
        out_specs=(vmem,) * 5,
        scratch_shapes=[
            pltpu.VMEM((FEAT, HID), BF16),
            pltpu.VMEM((ROWS, FEAT), BF16),
            pltpu.VMEM((ROWS, FEAT), BF16),
            pltpu.VMEM((SLOTS, RB, EMB), BF16),
            pltpu.VMEM((NC, RB, EMB), BF16),
            pltpu.VMEM((NC, RB, EMB), BF16),
            pltpu.VMEM((ROWS, HID), F32),
            pltpu.VMEM((ROWS, HID), F32),
            pltpu.VMEM((ROWS, HID), BF16),
            pltpu.VMEM((TAB, EMB, ROWS), BF16),
            pltpu.VMEM((4, TAB // 2, EB, ROWS), BF16),
            pltpu.VMEM((TAB // 2, EB, EMB), BF16),
            pltpu.VMEM((TAB // 2, EB, EMB), BF16),
            pltpu.VMEM((TAB, EB, EMB), BF16),
            pltpu.VMEM((TAB, EB, EMB), BF16),
            pltpu.VMEM((TAB // 2, EB, ROWS), BF16),
            pltpu.VMEM((TAB // 2, EB, ROWS), BF16),
            pltpu.VMEM((TAB // 2, EB, ROWS), BF16),
            pltpu.VMEM((TAB, EB, ROWS), BF16),
            pltpu.VMEM((TAB, EB, ROWS), BF16),
            pltpu.VMEM((TAB + 1, EB, ROWS), BF16),
            pltpu.VMEM((SLOTS, EB, ROWS), BF16),
            pltpu.VMEM((LOCAL, EMB, ROWS), BF16),
            pltpu.VMEM((1, ROWS), F32),
            pltpu.VMEM((NT, 1, ROWS), F32),
            pltpu.VMEM((1, ROWS), F32),
            pltpu.VMEM((NT, 1, ROWS), F32),
            pltpu.VMEM((1, ROWS), F32),
            pltpu.VMEM((NC, 1, ROWS), F32),
            pltpu.VMEM((1, HID), BF16),
            pltpu.VMEM((1, HID), BF16),
            pltpu.VMEM((1, ROWS), jnp.int32),
            pltpu.SMEM((TAB,), jnp.int32),
            pltpu.SMEM((NC,), jnp.int32),
            pltpu.VMEM((SLOTS, EMB), jnp.int32),
            pltpu.SMEM((SLOTS, EMB), jnp.int32),
            pltpu.SemaphoreType.REGULAR, pltpu.SemaphoreType.REGULAR,
            dma((6,)), dma,
            dma((NT,)), dma,
            tree, tree,
            dma((TAB,)), dma,
            dma((NC,)), dma,
            tree, tree,
            dma((NT,)), dma,
            dma((NT,)), dma,
            dma((NC,)), dma,
            tree, tree,
            dma((NT,)), dma,
        ],
        compiler_params=pltpu.CompilerParams(
            collective_id=0, has_side_effects=True, vmem_limit_bytes=40 * 1024 * 1024
        ),
    )(
        *(
            pltpu.with_memory_space_constraint(v, pltpu.HBM)
            for v in (
                slot_of_table, partner, labels.reshape(1, ROWS), jnp.transpose(pooled, (1, 0, 2)),
                w_first.reshape(FEAT, HID), b_first, w_head,
            )
        )
    )
    pg, gf, gb, gh, loss = pl.pallas_call(
        finish,
        out_shape=(
            jax.ShapeDtypeStruct((LOCAL, EMB, ROWS), BF16),
            jax.ShapeDtypeStruct((FEAT, HID), BF16),
            jax.ShapeDtypeStruct((1, HID), F32),
            jax.ShapeDtypeStruct((1, HID), F32),
            jax.ShapeDtypeStruct((1,), F32),
        ),
        in_specs=[vmem] * 5,
        out_specs=(hbm, hbm, vmem, vmem, smem),
        scratch_shapes=[dma((2,))],
        compiler_params=pltpu.CompilerParams(vmem_limit_bytes=24 * 1024 * 1024),
    )(*results)
    return pg, gf[None], gb, gh, loss


def solution(mesh):
    in_specs = (
        P("copy", "table", None), P(), P(), P("copy"), P("copy", None, "table"), P("copy", "table"), P("copy", "table"),
    )
    out_specs = (
        P("table", None, "copy"), P("copy", None, "table"), P("copy", "table"), P("copy", "table"), P("copy"),
    )
    return jax.shard_map(on_device, mesh=mesh, in_specs=in_specs, out_specs=out_specs, check_vma=False)
```

```python
import jax
import jax.numpy as jnp
from jax import lax
from jax.experimental import pallas as pl
from jax.experimental.pallas import tpu as pltpu
from jax.sharding import PartitionSpec as P

MESH = pl.DeviceIdType.MESH
F32, BF16 = jnp.float32, jnp.bfloat16
NT, NC = 8, 32
TAB, EMB, SLOTS, LOCAL = 26, 128, 40, 5
ROWS, HID, FEAT = 256, 512, 3328
RB = ROWS // NT
EB = EMB // NT
CH = 256
NCHUNK = FEAT // CH
HALF = FEAT // 2

A, B, BOTH = (0, RB // 2), (RB // 2, RB // 2), (0, RB)
ALL, LOW, HIGH = (0, FEAT), (0, HALF), (HALF, HALF)
TREE = (
    ((0, 0), (0, 1), A, ALL, "y"),
    ((0, 0), (0, 1), B, ALL, "y"),
    ((0, 0), (3, 0), BOTH, ALL, "right"),
    ((0, 0), (1, 0), BOTH, ALL, "left"),
    ((0, 1), (3, 1), A, ALL, "right"),
    ((0, 1), (1, 1), A, ALL, "left"),
    ((3, 0), (2, 0), BOTH, LOW, "right"),
    ((1, 0), (2, 0), BOTH, HIGH, "left"),
    ((3, 0), (3, 1), B, ALL, "y"),
    ((1, 0), (1, 1), B, ALL, "y"),
    ((3, 1), (2, 1), A, LOW, "right"),
    ((1, 1), (2, 1), A, HIGH, "left"),
    ((2, 0), (2, 1), B, ALL, "y"),
)
TREE_STEPS = (((), (0, 2, 3, 1)), ((0,), (4, 5)), ((2,), (6, 8)), ((3,), (7, 9)), ((4,), (10,)), ((5,), (11,)), ((6, 7), (12,)),
              ((1, 8, 9, 10, 11, 12), ()))


def relay_copy(r):
    return 2 * (r + jnp.where(r >= 5, 1, 0) + jnp.where(r >= 9, 1, 0))


def kernel(
    slot_h, partner_h, labels_h, pooled, w_hbm, b_h, h_h,
    ft_out, low_out, pg_out, gb_out, gh_out, loss_out,
    w_v, feat, feat_t, by_slot, relay_in, relay_out, act_v, a32_v, low_v, gt_v, in_b, in_a1, in_a2, in_low, in_high, in_al, in_ar,
    in_ay, in_l, in_r, sums, placed, pg_in,
    z_own, z_in, q_own, q_in, qs_own, qs_in, b_v, h_v, y_v, slot_s, partner_s, inv_v, inv_s,
    in_sem, go_sem, load_sem, inv_sem,
    a_send, a_recv, ag_send, ag_recv, c_send, c_recv, d_send, d_recv, tg_send, tg_recv,
    l_send, l_recv, m_send, m_recv, t_send, t_recv, r_send, r_recv, z_send, z_recv,
):
    c = lax.axis_index("copy")
    k = lax.axis_index("table")
    x, y = lax.rem(k, 4), k // 4
    my_rows = pl.ds(pl.multiple_of(k * RB, RB), RB)
    chip = c // 2
    is_relay = (lax.rem(c, 2) == 0) & (chip != 5) & (chip != 10) & (chip != 15)
    my_r = jnp.where(is_relay, chip - jnp.where(chip >= 5, 1, 0) - jnp.where(chip >= 10, 1, 0), 0)

    barrier = pltpu.get_barrier_semaphore()

    is_gate = k == 0

    def signal(sem, copy, table):
        pl.semaphore_signal(sem, inc=1, device_id=(copy, table), device_id_type=MESH)

    def greet_table(d, _):
        j = lax.rem(k + d, NT)

        @pl.when(j != 0)
        def _():
            signal(barrier, c, j)

        return 0

    lax.fori_loop(1, NT, greet_table, 0)

    loads = [
        pltpu.make_async_copy(src, dst, load_sem.at[i])
        for i, (src, dst) in enumerate(
            ((slot_h, slot_s), (partner_h, partner_s), (labels_h, y_v), (b_h, b_v), (h_h, h_v), (w_hbm, w_v))
        )
    ]
    for load in loads:
        load.start()

    @pl.when(jnp.logical_not(is_gate))
    def _():
        pl.semaphore_wait(barrier, NT - 1)
        signal(in_sem, c, 0)

    @pl.when(is_gate)
    def _():
        pl.semaphore_wait(in_sem, NT - 1)

        def greet_copy(d, _):
            signal(barrier, lax.rem(c + d, NC), k)
            return 0

        lax.fori_loop(1, NC, greet_copy, 0)

    def all_in():
        @pl.when(is_gate)
        def _():
            pl.semaphore_wait(barrier, NC - 1)
            for j in range(1, NT):
                signal(go_sem, c, j)

        @pl.when(jnp.logical_not(is_gate))
        def _():
            pl.semaphore_wait(go_sem, 1)

    def remote(src, dst, send, recv, copy, table):
        return pltpu.make_async_remote_copy(
            src_ref=src, dst_ref=dst, send_sem=send, recv_sem=recv, device_id=(copy, table), device_id_type=MESH
        )

    def over_table(fn):
        def body(d, _):
            fn(d, lax.rem(k + d, NT))
            return 0

        lax.fori_loop(1, NT, body, 0)

    def take(ref, sem):
        pltpu.make_async_copy(ref, ref, sem).wait()

    def share(step):
        return lax.rem(y + step[1], 2) * 4 + lax.rem(x + step[0], 4)

    target = {"y": share((0, 1)), "right": share((1, 0)), "left": share((3, 0))}

    def region(buf, origin, rows, cols):
        first = pl.multiple_of(share(origin) * RB + rows[0], RB // 2)
        return buf.at[pl.ds(first, rows[1]), pl.ds(cols[0], cols[1])]

    def tree_copy(buf, send, recv, i):
        origin, _, rows, cols, to = TREE[i]
        piece = region(buf, origin, rows, cols)
        return remote(piece, piece, send.at[i], recv.at[i], c, target[to])

    def tree_step(buf, send, recv, step):
        waits, starts = TREE_STEPS[step]
        for i in waits:
            _, origin, rows, cols, _ = TREE[i]
            take(region(buf, origin, rows, cols), recv.at[i])
        for i in starts:
            tree_copy(buf, send, recv, i).start()

    def a_copy(d, j):
        rows = pl.ds(pl.multiple_of(j * RB, RB), RB)
        return remote(pooled.at[:, rows, :], by_slot.at[pl.ds(k * LOCAL, LOCAL)], a_send.at[d], a_recv, c, j)

    over_table(lambda d, j: a_copy(d, j).start())
    pltpu.make_async_copy(pooled.at[:, my_rows, :], by_slot.at[pl.ds(k * LOCAL, LOCAL)], a_recv).start()
    for load in loads:
        load.wait()

    lane = lax.broadcasted_iota(jnp.int32, (8, EMB), 1)
    slots = jnp.full((8, EMB), SLOTS, jnp.int32)
    for t in range(TAB):
        slots = jnp.where(lane == t, slot_s[t], slots)
    for i in range(SLOTS // 8):
        found = jnp.where(lax.broadcasted_iota(jnp.int32, (8, EMB), 0) + 8 * i == slots, lane, TAB)
        inv_v[8 * i : 8 * i + 8, :] = jnp.broadcast_to(jnp.min(found, axis=1, keepdims=True), (8, EMB))
    inv_copy = pltpu.make_async_copy(inv_v, inv_s, inv_sem)
    inv_copy.start()

    take(by_slot, a_recv)
    for t in range(TAB):
        feat[my_rows, t * EMB : (t + 1) * EMB] = by_slot[slot_s[t]]

    tree_step(feat, ag_send, ag_recv, 0)

    def c_copy(i):
        r = lax.rem(i + my_r, NCHUNK)
        to = relay_copy(r)
        src = feat.at[my_rows, pl.ds(pl.multiple_of(r * CH, CH), CH)]
        return src, to, remote(src, relay_in.at[c], c_send.at[i], c_recv, to, k)

    def c_start(i, _):
        src, to, copy = c_copy(i)

        @pl.when(to != c)
        def _():
            copy.start()

        @pl.when(to == c)
        def _():
            pltpu.make_async_copy(src, relay_in.at[c], c_recv).start()

        return 0

    all_in()
    lax.fori_loop(0, NCHUNK, c_start, 0)
    for step in range(1, 6):
        tree_step(feat, ag_send, ag_recv, step)

    my_cols = pl.ds(pl.multiple_of(my_r * CH, CH), CH)

    def d_copy(d, p):
        return remote(relay_out.at[p], feat_t.at[my_rows, my_cols], d_send.at[d], d_recv, p, k)

    @pl.when(is_relay)
    def _():
        take(relay_in, c_recv)

        def pick(p, _):
            relay_out[p] = relay_in[partner_s[p]]
            return 0

        lax.fori_loop(0, NC, pick, 0, unroll=4)

        def d_start(d, _):
            d_copy(d, lax.rem(c + d, NC)).start()
            return 0

        lax.fori_loop(1, NC, d_start, 0)
        pltpu.make_async_copy(relay_out.at[c], feat_t.at[my_rows, my_cols], d_recv).start()

    for step in range(6, len(TREE_STEPS)):
        tree_step(feat, ag_send, ag_recv, step)

    def head_row(total):
        return jnp.sum(jnp.transpose(total), axis=0, keepdims=True)

    total = jnp.zeros((ROWS, EMB), F32)
    for n in range(HID // CH):
        cols = slice(n * CH, (n + 1) * CH)
        head = h_v[:, cols].astype(F32)
        pre = jnp.dot(feat[...], w_v[:, cols], preferred_element_type=F32) + b_v[:, cols].astype(F32)
        sig = jax.nn.sigmoid(pre)
        act = pre * sig
        act_v[:, cols] = act
        a32 = head * (sig * (1.0 + pre * (1.0 - sig)))
        a32_v[:, cols] = a32
        low_v[:, cols] = a32.astype(BF16)
        weighed = act * head
        total = total + (weighed[:, :EMB] + weighed[:, EMB:])
    z_own[...] = head_row(total)

    z_in[k] = z_own[...]

    def l_copy(d, j):
        return remote(z_own, z_in.at[k], l_send.at[d], l_recv, c, j)

    over_table(lambda d, j: l_copy(d, j).start())

    def partials():
        def gt_step(i, _):
            rows = pl.ds(pl.multiple_of(i * CH, CH), CH)
            g = lax.dot_general(w_v[rows, :], low_v[...], (((1,), (1,)), ((), ())), preferred_element_type=F32)
            gt_v[pl.ds(i * 2, 2)] = g.astype(BF16).reshape(2, EMB, ROWS)
            return 0

        lax.fori_loop(0, NCHUNK, gt_step, 0)

    def part(step, tables=(0, TAB), lanes=(0, ROWS)):
        first = pl.multiple_of(share(step) * EB, EB)
        return pl.ds(tables[0], tables[1]), pl.ds(first, EB), pl.ds(lanes[0], lanes[1])

    ta, tb, every = (0, TAB // 2), (TAB // 2, TAB // 2), (0, TAB)
    low, high, full = (0, EMB), (EMB, EMB), (0, ROWS)
    messages = (
        ((2, 1), tb, full, in_b.at[0], "y"),
        ((2, 1), ta, low, in_a1, "left"),
        ((2, 1), ta, high, in_a2, "right"),
        ((3, 1), tb, full, in_b.at[1], "y"),
        ((1, 1), tb, full, in_b.at[2], "y"),
        ((0, 1), tb, full, in_b.at[3], "y"),
        ((2, 0), every, low, in_low, "left"),
        ((2, 0), every, high, in_high, "right"),
        ((3, 1), ta, full, in_al, "left"),
        ((1, 1), ta, full, in_ar, "right"),
        ((3, 0), every, full, in_l, "left"),
        ((1, 0), every, full, in_r, "right"),
        ((0, 1), ta, full, in_ay, "y"),
    )

    def reduce_copy(i):
        step, tables, lanes, dst, to = messages[i]
        return remote(gt_v.at[part(step, tables, lanes)], dst, r_send.at[i], r_recv.at[i], c, target[to])

    def add(step, tables, lanes, *arrived):
        where = part(step, tables, lanes)
        total = gt_v[where].astype(F32)
        for ref, i in arrived:
            take(ref, r_recv.at[i])
            total = total + ref[...].astype(F32)
        gt_v[where] = total.astype(BF16)

    def reduce_leaves():
        for i in range(6):
            reduce_copy(i).start()

    def reduce_first():
        add((2, 0), tb, full, (in_b.at[0], 0))
        reduce_copy(6).start()
        reduce_copy(7).start()
        add((3, 1), ta, low, (in_a1, 1))
        reduce_copy(8).start()
        add((1, 1), ta, high, (in_a2, 2))
        reduce_copy(9).start()

    def reduce_second():
        add((3, 0), tb, full, (in_b.at[1], 3))
        add((3, 0), every, low, (in_low, 6))
        reduce_copy(10).start()
        add((1, 0), tb, full, (in_b.at[2], 4))
        add((1, 0), every, high, (in_high, 7))
        reduce_copy(11).start()
        add((0, 1), ta, full, (in_al, 8), (in_ar, 9))
        reduce_copy(12).start()

    ahead = c < NC // 2
    behind = jnp.logical_not(ahead)

    @pl.when(ahead)
    def _():
        partials()
        reduce_leaves()
        reduce_first()

    take(feat_t.at[my_rows], d_recv)
    tree_step(feat_t, tg_send, tg_recv, 0)

    @pl.when(behind)
    def _():
        partials()


    for step in range(1, 7):
        tree_step(feat_t, tg_send, tg_recv, step)

    @pl.when(behind)
    def _():
        reduce_leaves()

    @pl.when(ahead)
    def _():
        reduce_second()

    tree_step(feat_t, tg_send, tg_recv, 7)
    @pl.when(behind)
    def _():
        reduce_first()

    total = jnp.zeros((ROWS, EMB), F32)
    for n in range(HID // CH):
        cols = slice(n * CH, (n + 1) * CH)
        pre = jnp.dot(feat_t[...], w_v[:, cols], preferred_element_type=F32) + b_v[:, cols].astype(F32)
        weighed = pre * jax.nn.sigmoid(pre) * h_v[:, cols].astype(F32)
        total = total + (weighed[:, :EMB] + weighed[:, EMB:])
    q_own[...] = head_row(total)
    q_in[k] = q_own[...]

    def m_copy(d, j):
        return remote(q_own, q_in.at[k], m_send.at[d], m_recv, c, j)

    over_table(lambda d, j: m_copy(d, j).start())

    take(z_in.at[pl.ds(0, NT - 1)], l_recv)
    take(q_in.at[pl.ds(0, NT - 1)], m_recv)
    qs_own[...] = jnp.sum(q_in[...], axis=0)
    qs_in[c] = qs_own[...]

    def t_copy(d):
        return remote(qs_own, qs_in.at[c], t_send.at[d], t_recv, lax.rem(c + d, NC), k)

    def t_start(d, _):
        t_copy(d).start()
        return 0

    lax.fori_loop(1, NC, t_start, 0)

    @pl.when(behind)
    def _():
        reduce_second()

    for ref, i in ((in_b.at[3], 5), (in_l, 10), (in_r, 11), (in_ay, 12)):
        take(ref, r_recv.at[i])
    inv_copy.wait()
    mine = pl.ds(pl.multiple_of(k * EB, EB), EB)
    half = TAB // 2
    total = gt_v[0:half, mine, :].astype(F32) + in_ay[...].astype(F32)
    total = total + in_l[0:half].astype(F32) + in_r[0:half].astype(F32)
    sums[0:half] = total.astype(BF16)
    total = gt_v[half:TAB, mine, :].astype(F32) + in_b[3].astype(F32)
    total = total + in_l[half:TAB].astype(F32) + in_r[half:TAB].astype(F32)
    sums[half:TAB] = total.astype(BF16)
    sums[TAB] = jnp.zeros((EB, ROWS), BF16)

    def place(s, _):
        placed[s] = sums[inv_s[s, 0]]
        return 0

    lax.fori_loop(0, SLOTS, place, 0, unroll=4)

    def z_copy(d, j):
        return remote(placed.at[pl.ds(j * LOCAL, LOCAL)], pg_in.at[:, mine, :], z_send.at[d], z_recv, c, j)

    over_table(lambda d, j: z_copy(d, j).start())
    pltpu.make_async_copy(placed.at[pl.ds(k * LOCAL, LOCAL)], pg_in.at[:, mine, :], z_recv).start()

    def flip(i, _):
        rows = pl.ds(pl.multiple_of(i * CH, CH), CH)
        ft_out[rows, :] = jnp.transpose(feat[:, rows])
        return 0

    lax.fori_loop(0, NCHUNK, flip, 0)

    take(qs_in.at[pl.ds(0, NC - 1)], t_recv)
    z = jnp.sum(z_in[...], axis=0)
    q = jax.nn.sigmoid(qs_in[partner_s[c]])
    target_y = y_v[...].astype(F32)
    soft = jnp.maximum(z, 0.0) + jnp.log1p(jnp.exp(-jnp.abs(z)))
    lg = 2.0 * jax.nn.sigmoid(z) - target_y - q
    loss_out[...] = jnp.broadcast_to(
        jnp.sum(2.0 * soft - target_y * z - q * z, axis=1, keepdims=True) * (1.0 / ROWS), (1, EMB)
    )
    lg_col = jnp.transpose(jnp.broadcast_to(lg, (EMB, ROWS)))
    for n in range(HID // EMB):
        cols = slice(n * EMB, (n + 1) * EMB)
        grad_pre = lg_col * a32_v[:, cols]
        low_out[:, cols] = grad_pre.astype(BF16)
        gb_out[:, cols] = jnp.sum(grad_pre, axis=0, keepdims=True)
        gh_out[:, cols] = jnp.sum(lg_col * act_v[:, cols], axis=0, keepdims=True)

    take(pg_in, z_recv)
    for e in range(LOCAL):
        pg_out[e] = (pg_in[e].astype(F32) * lg).astype(BF16)

    over_table(lambda d, j: a_copy(d, j).wait_send())

    def c_wait(i, _):
        _, to, copy = c_copy(i)

        @pl.when(to != c)
        def _():
            copy.wait_send()

        return 0

    lax.fori_loop(0, NCHUNK, c_wait, 0)
    for i in range(len(TREE)):
        tree_copy(feat, ag_send, ag_recv, i).wait_send()
        tree_copy(feat_t, tg_send, tg_recv, i).wait_send()

    @pl.when(is_relay)
    def _():
        def d_wait(d, _):
            d_copy(d, lax.rem(c + d, NC)).wait_send()
            return 0

        lax.fori_loop(1, NC, d_wait, 0)

    def t_wait(d, _):
        t_copy(d).wait_send()
        return 0

    lax.fori_loop(1, NC, t_wait, 0)

    def rest(d, j):
        l_copy(d, j).wait_send()
        m_copy(d, j).wait_send()
        z_copy(d, j).wait_send()

    over_table(rest)
    for i in range(len(messages)):
        reduce_copy(i).wait_send()


def finish(ft_v, low_v, pg_v, gb_v, gh_v, loss_v, pg_out, gf_out, gb_out, gh_out, loss_out, gf_v, gf_sem, pg_sem):
    pg_copy = pltpu.make_async_copy(pg_v, pg_out, pg_sem)
    pg_copy.start()
    copies = []
    for i in range(NCHUNK):
        rows = pl.ds(i * CH, CH)
        gf_v[rows, :] = jnp.dot(ft_v[rows, :], low_v[...], preferred_element_type=F32).astype(BF16)
        copy = pltpu.make_async_copy(gf_v.at[rows], gf_out.at[rows], gf_sem.at[i])
        copy.start()
        copies.append(copy)
    gb_out[...] = gb_v[...]
    gh_out[...] = gh_v[...]
    loss_out[0] = jnp.sum(loss_v[:, 0:1])
    pg_copy.wait()
    for copy in copies:
        copy.wait()


def on_device(pooled, slot_of_table, partner, labels, w_first, b_first, w_head):
    vmem = pl.BlockSpec(memory_space=pltpu.VMEM)
    smem = pl.BlockSpec(memory_space=pltpu.SMEM)
    hbm = pl.BlockSpec(memory_space=pltpu.HBM)
    dma = pltpu.SemaphoreType.DMA
    tree = dma((len(TREE),))
    results = pl.pallas_call(
        kernel,
        out_shape=(
            jax.ShapeDtypeStruct((FEAT, ROWS), BF16),
            jax.ShapeDtypeStruct((ROWS, HID), BF16),
            jax.ShapeDtypeStruct((LOCAL, EMB, ROWS), BF16),
            jax.ShapeDtypeStruct((1, HID), F32),
            jax.ShapeDtypeStruct((1, HID), F32),
            jax.ShapeDtypeStruct((1, EMB), F32),
        ),
        in_specs=[hbm] * 7,
        out_specs=(vmem,) * 6,
        scratch_shapes=[
            pltpu.VMEM((FEAT, HID), BF16),
            pltpu.VMEM((ROWS, FEAT), BF16),
            pltpu.VMEM((ROWS, FEAT), BF16),
            pltpu.VMEM((SLOTS, RB, EMB), BF16),
            pltpu.VMEM((NC, RB, CH), BF16),
            pltpu.VMEM((NC, RB, CH), BF16),
            pltpu.VMEM((ROWS, HID), F32),
            pltpu.VMEM((ROWS, HID), F32),
            pltpu.VMEM((ROWS, HID), BF16),
            pltpu.VMEM((TAB, EMB, ROWS), BF16),
            pltpu.VMEM((4, TAB // 2, EB, ROWS), BF16),
            pltpu.VMEM((TAB // 2, EB, EMB), BF16),
            pltpu.VMEM((TAB // 2, EB, EMB), BF16),
            pltpu.VMEM((TAB, EB, EMB), BF16),
            pltpu.VMEM((TAB, EB, EMB), BF16),
            pltpu.VMEM((TAB // 2, EB, ROWS), BF16),
            pltpu.VMEM((TAB // 2, EB, ROWS), BF16),
            pltpu.VMEM((TAB // 2, EB, ROWS), BF16),
            pltpu.VMEM((TAB, EB, ROWS), BF16),
            pltpu.VMEM((TAB, EB, ROWS), BF16),
            pltpu.VMEM((TAB + 1, EB, ROWS), BF16),
            pltpu.VMEM((SLOTS, EB, ROWS), BF16),
            pltpu.VMEM((LOCAL, EMB, ROWS), BF16),
            pltpu.VMEM((1, ROWS), F32),
            pltpu.VMEM((NT, 1, ROWS), F32),
            pltpu.VMEM((1, ROWS), F32),
            pltpu.VMEM((NT, 1, ROWS), F32),
            pltpu.VMEM((1, ROWS), F32),
            pltpu.VMEM((NC, 1, ROWS), F32),
            pltpu.VMEM((1, HID), BF16),
            pltpu.VMEM((1, HID), BF16),
            pltpu.VMEM((1, ROWS), jnp.int32),
            pltpu.SMEM((TAB,), jnp.int32),
            pltpu.SMEM((NC,), jnp.int32),
            pltpu.VMEM((SLOTS, EMB), jnp.int32),
            pltpu.SMEM((SLOTS, EMB), jnp.int32),
            pltpu.SemaphoreType.REGULAR, pltpu.SemaphoreType.REGULAR,
            dma((6,)), dma,
            dma((NT,)), dma,
            tree, tree,
            dma((NCHUNK,)), dma,
            dma((NC,)), dma,
            tree, tree,
            dma((NT,)), dma,
            dma((NT,)), dma,
            dma((NC,)), dma,
            tree, tree,
            dma((NT,)), dma,
        ],
        compiler_params=pltpu.CompilerParams(
            collective_id=0, has_side_effects=True, vmem_limit_bytes=40 * 1024 * 1024
        ),
    )(
        *(
            pltpu.with_memory_space_constraint(v, pltpu.HBM)
            for v in (
                slot_of_table, partner, labels.reshape(1, ROWS), jnp.transpose(pooled, (1, 0, 2)),
                w_first.reshape(FEAT, HID), b_first, w_head,
            )
        )
    )
    pg, gf, gb, gh, loss = pl.pallas_call(
        finish,
        out_shape=(
            jax.ShapeDtypeStruct((LOCAL, EMB, ROWS), BF16),
            jax.ShapeDtypeStruct((FEAT, HID), BF16),
            jax.ShapeDtypeStruct((1, HID), F32),
            jax.ShapeDtypeStruct((1, HID), F32),
            jax.ShapeDtypeStruct((1,), F32),
        ),
        in_specs=[vmem] * 6,
        out_specs=(hbm, hbm, vmem, vmem, smem),
        scratch_shapes=[pltpu.VMEM((FEAT, HID), BF16), dma((NCHUNK,)), dma],
        compiler_params=pltpu.CompilerParams(vmem_limit_bytes=24 * 1024 * 1024),
    )(*results)
    return pg, gf[None], gb, gh, loss


def solution(mesh):
    in_specs = (
        P("copy", "table", None), P(), P(), P("copy"), P("copy", None, "table"), P("copy", "table"), P("copy", "table"),
    )
    out_specs = (
        P("table", None, "copy"), P("copy", None, "table"), P("copy", "table"), P("copy", "table"), P("copy"),
    )
    return jax.shard_map(on_device, mesh=mesh, in_specs=in_specs, out_specs=out_specs, check_vma=False)
```

```python
import jax
import jax.numpy as jnp
from jax import lax
from jax.experimental import pallas as pl
from jax.experimental.pallas import tpu as pltpu
from jax.sharding import PartitionSpec as P

MESH = pl.DeviceIdType.MESH
F32, BF16 = jnp.float32, jnp.bfloat16
NT, NC = 8, 32
TAB, EMB, SLOTS, LOCAL = 26, 128, 40, 5
ROWS, HID, FEAT = 256, 512, 3328
RB = ROWS // NT
EB = EMB // NT
CH = 256
NCHUNK = FEAT // CH
HALF = FEAT // 2

A, B, BOTH = (0, RB // 2), (RB // 2, RB // 2), (0, RB)
ALL, LOW, HIGH = (0, FEAT), (0, HALF), (HALF, HALF)
TREE = (
    ((0, 0), (0, 1), A, ALL, "y"),
    ((0, 0), (0, 1), B, ALL, "y"),
    ((0, 0), (3, 0), BOTH, ALL, "right"),
    ((0, 0), (1, 0), BOTH, ALL, "left"),
    ((0, 1), (3, 1), A, ALL, "right"),
    ((0, 1), (1, 1), A, ALL, "left"),
    ((3, 0), (2, 0), BOTH, LOW, "right"),
    ((1, 0), (2, 0), BOTH, HIGH, "left"),
    ((3, 0), (3, 1), B, ALL, "y"),
    ((1, 0), (1, 1), B, ALL, "y"),
    ((3, 1), (2, 1), A, LOW, "right"),
    ((1, 1), (2, 1), A, HIGH, "left"),
    ((2, 0), (2, 1), B, ALL, "y"),
)
TREE_STEPS = (((), (0, 2, 3, 1)), ((0,), (4, 5)), ((2,), (6, 8)), ((3,), (7, 9)), ((4,), (10,)), ((5,), (11,)), ((6, 7), (12,)),
              ((1, 8, 9, 10, 11, 12), ()))


def relay_copy(r):
    return 2 * (r + jnp.where(r >= 5, 1, 0) + jnp.where(r >= 9, 1, 0))


def kernel(
    slot_h, partner_h, labels_h, pooled, w_hbm, b_h, h_h,
    ft_out, low_out, pg_out, gb_out, gh_out, loss_out,
    w_v, feat, feat_t, by_slot, relay_in, relay_out, act_v, a32_v, low_v, gt_v, in_b, in_a1, in_a2, in_low, in_high, in_al, in_ar,
    in_ay, in_l, in_r, sums, placed, pg_in,
    z_own, z_in, q_own, q_in, qs_own, qs_in, b_v, h_v, y_v, slot_s, partner_s, inv_v, inv_s,
    in_sem, go_sem, load_sem, inv_sem,
    a_send, a_recv, ag_send, ag_recv, c_send, c_recv, d_send, d_recv, tg_send, tg_recv,
    l_send, l_recv, m_send, m_recv, t_send, t_recv, r_send, r_recv, z_send, z_recv,
):
    c = lax.axis_index("copy")
    k = lax.axis_index("table")
    x, y = lax.rem(k, 4), k // 4
    my_rows = pl.ds(pl.multiple_of(k * RB, RB), RB)
    chip = c // 2
    is_relay = (lax.rem(c, 2) == 0) & (chip != 5) & (chip != 10) & (chip != 15)
    my_r = jnp.where(is_relay, chip - jnp.where(chip >= 5, 1, 0) - jnp.where(chip >= 10, 1, 0), 0)

    barrier = pltpu.get_barrier_semaphore()

    is_gate = k == 0

    def signal(sem, copy, table):
        pl.semaphore_signal(sem, inc=1, device_id=(copy, table), device_id_type=MESH)

    def greet_table(d, _):
        j = lax.rem(k + d, NT)

        @pl.when(j != 0)
        def _():
            signal(barrier, c, j)

        return 0

    lax.fori_loop(1, NT, greet_table, 0)

    loads = [
        pltpu.make_async_copy(src, dst, load_sem.at[i])
        for i, (src, dst) in enumerate(
            ((slot_h, slot_s), (partner_h, partner_s), (labels_h, y_v), (b_h, b_v), (h_h, h_v), (w_hbm, w_v))
        )
    ]
    for load in loads:
        load.start()

    @pl.when(jnp.logical_not(is_gate))
    def _():
        pl.semaphore_wait(barrier, NT - 1)
        signal(in_sem, c, 0)

    @pl.when(is_gate)
    def _():
        pl.semaphore_wait(in_sem, NT - 1)

        def greet_copy(d, _):
            signal(barrier, lax.rem(c + d, NC), k)
            return 0

        lax.fori_loop(1, NC, greet_copy, 0)

    def all_in():
        @pl.when(is_gate)
        def _():
            pl.semaphore_wait(barrier, NC - 1)
            for j in range(1, NT):
                signal(go_sem, c, j)

        @pl.when(jnp.logical_not(is_gate))
        def _():
            pl.semaphore_wait(go_sem, 1)

    def remote(src, dst, send, recv, copy, table):
        return pltpu.make_async_remote_copy(
            src_ref=src, dst_ref=dst, send_sem=send, recv_sem=recv, device_id=(copy, table), device_id_type=MESH
        )

    def over_table(fn):
        def body(d, _):
            fn(d, lax.rem(k + d, NT))
            return 0

        lax.fori_loop(1, NT, body, 0)

    def take(ref, sem):
        pltpu.make_async_copy(ref, ref, sem).wait()

    def share(step):
        return lax.rem(y + step[1], 2) * 4 + lax.rem(x + step[0], 4)

    target = {"y": share((0, 1)), "right": share((1, 0)), "left": share((3, 0))}

    def region(buf, origin, rows, cols):
        first = pl.multiple_of(share(origin) * RB + rows[0], RB // 2)
        return buf.at[pl.ds(first, rows[1]), pl.ds(cols[0], cols[1])]

    def tree_copy(buf, send, recv, i):
        origin, _, rows, cols, to = TREE[i]
        piece = region(buf, origin, rows, cols)
        return remote(piece, piece, send.at[i], recv.at[i], c, target[to])

    def tree_step(buf, send, recv, step):
        waits, starts = TREE_STEPS[step]
        for i in waits:
            _, origin, rows, cols, _ = TREE[i]
            take(region(buf, origin, rows, cols), recv.at[i])
        for i in starts:
            tree_copy(buf, send, recv, i).start()

    def a_copy(d, j):
        rows = pl.ds(pl.multiple_of(j * RB, RB), RB)
        return remote(pooled.at[:, rows, :], by_slot.at[pl.ds(k * LOCAL, LOCAL)], a_send.at[d], a_recv, c, j)

    over_table(lambda d, j: a_copy(d, j).start())
    pltpu.make_async_copy(pooled.at[:, my_rows, :], by_slot.at[pl.ds(k * LOCAL, LOCAL)], a_recv).start()
    for load in loads:
        load.wait()

    lane = lax.broadcasted_iota(jnp.int32, (8, EMB), 1)
    slots = jnp.full((8, EMB), SLOTS, jnp.int32)
    for t in range(TAB):
        slots = jnp.where(lane == t, slot_s[t], slots)
    for i in range(SLOTS // 8):
        found = jnp.where(lax.broadcasted_iota(jnp.int32, (8, EMB), 0) + 8 * i == slots, lane, TAB)
        inv_v[8 * i : 8 * i + 8, :] = jnp.broadcast_to(jnp.min(found, axis=1, keepdims=True), (8, EMB))
    inv_copy = pltpu.make_async_copy(inv_v, inv_s, inv_sem)
    inv_copy.start()

    take(by_slot, a_recv)
    for t in range(TAB):
        feat[my_rows, t * EMB : (t + 1) * EMB] = by_slot[slot_s[t]]

    tree_step(feat, ag_send, ag_recv, 0)

    def c_copy(i):
        r = lax.rem(i + my_r, NCHUNK)
        to = relay_copy(r)
        src = feat.at[my_rows, pl.ds(pl.multiple_of(r * CH, CH), CH)]
        return src, to, remote(src, relay_in.at[c], c_send.at[i], c_recv, to, k)

    def c_start(i, _):
        src, to, copy = c_copy(i)

        @pl.when(to != c)
        def _():
            copy.start()

        @pl.when(to == c)
        def _():
            pltpu.make_async_copy(src, relay_in.at[c], c_recv).start()

        return 0

    all_in()
    lax.fori_loop(0, NCHUNK, c_start, 0)
    for step in range(1, 7):
        tree_step(feat, ag_send, ag_recv, step)

    my_cols = pl.ds(pl.multiple_of(my_r * CH, CH), CH)

    def d_copy(d, p):
        return remote(relay_out.at[p], feat_t.at[my_rows, my_cols], d_send.at[d], d_recv, p, k)

    @pl.when(is_relay)
    def _():
        take(relay_in, c_recv)

        def pick(p, _):
            relay_out[p] = relay_in[partner_s[p]]
            return 0

        lax.fori_loop(0, NC, pick, 0, unroll=4)

        def d_start(d, _):
            d_copy(d, lax.rem(c + d, NC)).start()
            return 0

        lax.fori_loop(1, NC, d_start, 0)
        pltpu.make_async_copy(relay_out.at[c], feat_t.at[my_rows, my_cols], d_recv).start()

    tree_step(feat, ag_send, ag_recv, 7)

    def head_row(total):
        return jnp.sum(jnp.transpose(total), axis=0, keepdims=True)

    total = jnp.zeros((ROWS, EMB), F32)
    for n in range(HID // CH):
        cols = slice(n * CH, (n + 1) * CH)
        head = h_v[:, cols].astype(F32)
        pre = jnp.dot(feat[...], w_v[:, cols], preferred_element_type=F32) + b_v[:, cols].astype(F32)
        sig = jax.nn.sigmoid(pre)
        act = pre * sig
        act_v[:, cols] = act
        a32 = head * (sig * (1.0 + pre * (1.0 - sig)))
        a32_v[:, cols] = a32
        low_v[:, cols] = a32.astype(BF16)
        weighed = act * head
        total = total + (weighed[:, :EMB] + weighed[:, EMB:])
    z_own[...] = head_row(total)

    z_in[k] = z_own[...]

    def l_copy(d, j):
        return remote(z_own, z_in.at[k], l_send.at[d], l_recv, c, j)

    over_table(lambda d, j: l_copy(d, j).start())

    def partials():
        def gt_step(i, _):
            rows = pl.ds(pl.multiple_of(i * CH, CH), CH)
            g = lax.dot_general(w_v[rows, :], low_v[...], (((1,), (1,)), ((), ())), preferred_element_type=F32)
            gt_v[pl.ds(i * 2, 2)] = g.astype(BF16).reshape(2, EMB, ROWS)
            return 0

        lax.fori_loop(0, NCHUNK, gt_step, 0)

    def part(step, tables=(0, TAB), lanes=(0, ROWS)):
        first = pl.multiple_of(share(step) * EB, EB)
        return pl.ds(tables[0], tables[1]), pl.ds(first, EB), pl.ds(lanes[0], lanes[1])

    ta, tb, every = (0, TAB // 2), (TAB // 2, TAB // 2), (0, TAB)
    low, high, full = (0, EMB), (EMB, EMB), (0, ROWS)
    messages = (
        ((2, 1), tb, full, in_b.at[0], "y"),
        ((2, 1), ta, low, in_a1, "left"),
        ((2, 1), ta, high, in_a2, "right"),
        ((3, 1), tb, full, in_b.at[1], "y"),
        ((1, 1), tb, full, in_b.at[2], "y"),
        ((0, 1), tb, full, in_b.at[3], "y"),
        ((2, 0), every, low, in_low, "left"),
        ((2, 0), every, high, in_high, "right"),
        ((3, 1), ta, full, in_al, "left"),
        ((1, 1), ta, full, in_ar, "right"),
        ((3, 0), every, full, in_l, "left"),
        ((1, 0), every, full, in_r, "right"),
        ((0, 1), ta, full, in_ay, "y"),
    )

    def reduce_copy(i):
        step, tables, lanes, dst, to = messages[i]
        return remote(gt_v.at[part(step, tables, lanes)], dst, r_send.at[i], r_recv.at[i], c, target[to])

    def add(step, tables, lanes, *arrived):
        where = part(step, tables, lanes)
        total = gt_v[where].astype(F32)
        for ref, i in arrived:
            take(ref, r_recv.at[i])
            total = total + ref[...].astype(F32)
        gt_v[where] = total.astype(BF16)

    def reduce_leaves():
        for i in range(6):
            reduce_copy(i).start()

    def reduce_first():
        add((2, 0), tb, full, (in_b.at[0], 0))
        reduce_copy(6).start()
        reduce_copy(7).start()
        add((3, 1), ta, low, (in_a1, 1))
        reduce_copy(8).start()
        add((1, 1), ta, high, (in_a2, 2))
        reduce_copy(9).start()

    def reduce_second():
        add((3, 0), tb, full, (in_b.at[1], 3))
        add((3, 0), every, low, (in_low, 6))
        reduce_copy(10).start()
        add((1, 0), tb, full, (in_b.at[2], 4))
        add((1, 0), every, high, (in_high, 7))
        reduce_copy(11).start()
        add((0, 1), ta, full, (in_al, 8), (in_ar, 9))
        reduce_copy(12).start()

    ahead = c < NC // 2
    behind = jnp.logical_not(ahead)

    @pl.when(ahead)
    def _():
        partials()
        reduce_leaves()

    take(feat_t.at[my_rows], d_recv)
    tree_step(feat_t, tg_send, tg_recv, 0)

    @pl.when(ahead)
    def _():
        reduce_first()

    @pl.when(behind)
    def _():
        partials()


    for step in range(1, 7):
        tree_step(feat_t, tg_send, tg_recv, step)

    @pl.when(behind)
    def _():
        reduce_leaves()

    tree_step(feat_t, tg_send, tg_recv, 7)
    @pl.when(behind)
    def _():
        reduce_first()

    total = jnp.zeros((ROWS, EMB), F32)
    for n in range(HID // CH):
        cols = slice(n * CH, (n + 1) * CH)
        pre = jnp.dot(feat_t[...], w_v[:, cols], preferred_element_type=F32) + b_v[:, cols].astype(F32)
        weighed = pre * jax.nn.sigmoid(pre) * h_v[:, cols].astype(F32)
        total = total + (weighed[:, :EMB] + weighed[:, EMB:])
    q_own[...] = head_row(total)
    q_in[k] = q_own[...]

    def m_copy(d, j):
        return remote(q_own, q_in.at[k], m_send.at[d], m_recv, c, j)

    over_table(lambda d, j: m_copy(d, j).start())

    reduce_second()


    take(z_in.at[pl.ds(0, NT - 1)], l_recv)
    take(q_in.at[pl.ds(0, NT - 1)], m_recv)
    qs_own[...] = jnp.sum(q_in[...], axis=0)
    qs_in[c] = qs_own[...]

    def t_copy(d):
        return remote(qs_own, qs_in.at[c], t_send.at[d], t_recv, lax.rem(c + d, NC), k)

    def t_start(d, _):
        t_copy(d).start()
        return 0

    lax.fori_loop(1, NC, t_start, 0)


    for ref, i in ((in_b.at[3], 5), (in_l, 10), (in_r, 11), (in_ay, 12)):
        take(ref, r_recv.at[i])
    inv_copy.wait()
    mine = pl.ds(pl.multiple_of(k * EB, EB), EB)
    half = TAB // 2
    total = gt_v[0:half, mine, :].astype(F32) + in_ay[...].astype(F32)
    total = total + in_l[0:half].astype(F32) + in_r[0:half].astype(F32)
    sums[0:half] = total.astype(BF16)
    total = gt_v[half:TAB, mine, :].astype(F32) + in_b[3].astype(F32)
    total = total + in_l[half:TAB].astype(F32) + in_r[half:TAB].astype(F32)
    sums[half:TAB] = total.astype(BF16)
    sums[TAB] = jnp.zeros((EB, ROWS), BF16)

    def place(s, _):
        placed[s] = sums[inv_s[s, 0]]
        return 0

    lax.fori_loop(0, SLOTS, place, 0, unroll=4)

    def z_copy(d, j):
        return remote(placed.at[pl.ds(j * LOCAL, LOCAL)], pg_in.at[:, mine, :], z_send.at[d], z_recv, c, j)

    over_table(lambda d, j: z_copy(d, j).start())
    pltpu.make_async_copy(placed.at[pl.ds(k * LOCAL, LOCAL)], pg_in.at[:, mine, :], z_recv).start()

    def flip(i, _):
        rows = pl.ds(pl.multiple_of(i * CH, CH), CH)
        ft_out[rows, :] = jnp.transpose(feat[:, rows])
        return 0

    lax.fori_loop(0, NCHUNK, flip, 0)

    over_table(lambda d, j: a_copy(d, j).wait_send())

    def c_wait(i, _):
        _, to, copy = c_copy(i)

        @pl.when(to != c)
        def _():
            copy.wait_send()

        return 0

    lax.fori_loop(0, NCHUNK, c_wait, 0)
    for i in range(len(TREE)):
        tree_copy(feat, ag_send, ag_recv, i).wait_send()
        tree_copy(feat_t, tg_send, tg_recv, i).wait_send()

    @pl.when(is_relay)
    def _():
        def d_wait(d, _):
            d_copy(d, lax.rem(c + d, NC)).wait_send()
            return 0

        lax.fori_loop(1, NC, d_wait, 0)

    def t_wait(d, _):
        t_copy(d).wait_send()
        return 0

    lax.fori_loop(1, NC, t_wait, 0)

    def rest(d, j):
        l_copy(d, j).wait_send()
        m_copy(d, j).wait_send()
        z_copy(d, j).wait_send()

    over_table(rest)
    for i in range(len(messages)):
        reduce_copy(i).wait_send()

    take(qs_in.at[pl.ds(0, NC - 1)], t_recv)
    z = jnp.sum(z_in[...], axis=0)
    q = jax.nn.sigmoid(qs_in[partner_s[c]])
    target_y = y_v[...].astype(F32)
    soft = jnp.maximum(z, 0.0) + jnp.log1p(jnp.exp(-jnp.abs(z)))
    lg = 2.0 * jax.nn.sigmoid(z) - target_y - q
    loss_out[...] = jnp.broadcast_to(
        jnp.sum(2.0 * soft - target_y * z - q * z, axis=1, keepdims=True) * (1.0 / ROWS), (1, EMB)
    )
    lg_col = jnp.transpose(jnp.broadcast_to(lg, (EMB, ROWS)))
    for n in range(HID // EMB):
        cols = slice(n * EMB, (n + 1) * EMB)
        grad_pre = lg_col * a32_v[:, cols]
        low_out[:, cols] = grad_pre.astype(BF16)
        gb_out[:, cols] = jnp.sum(grad_pre, axis=0, keepdims=True)
        gh_out[:, cols] = jnp.sum(lg_col * act_v[:, cols], axis=0, keepdims=True)

    take(pg_in, z_recv)
    for e in range(LOCAL):
        pg_out[e] = (pg_in[e].astype(F32) * lg).astype(BF16)


def finish(ft_v, low_v, pg_v, gb_v, gh_v, loss_v, pg_out, gf_out, gb_out, gh_out, loss_out, gf_v, gf_sem, pg_sem):
    pg_copy = pltpu.make_async_copy(pg_v, pg_out, pg_sem)
    pg_copy.start()
    copies = []
    for i in range(NCHUNK):
        rows = pl.ds(i * CH, CH)
        gf_v[rows, :] = jnp.dot(ft_v[rows, :], low_v[...], preferred_element_type=F32).astype(BF16)
        copy = pltpu.make_async_copy(gf_v.at[rows], gf_out.at[rows], gf_sem.at[i])
        copy.start()
        copies.append(copy)
    gb_out[...] = gb_v[...]
    gh_out[...] = gh_v[...]
    loss_out[0] = jnp.sum(loss_v[:, 0:1])
    pg_copy.wait()
    for copy in copies:
        copy.wait()


def on_device(pooled, slot_of_table, partner, labels, w_first, b_first, w_head):
    vmem = pl.BlockSpec(memory_space=pltpu.VMEM)
    smem = pl.BlockSpec(memory_space=pltpu.SMEM)
    hbm = pl.BlockSpec(memory_space=pltpu.HBM)
    dma = pltpu.SemaphoreType.DMA
    tree = dma((len(TREE),))
    results = pl.pallas_call(
        kernel,
        out_shape=(
            jax.ShapeDtypeStruct((FEAT, ROWS), BF16),
            jax.ShapeDtypeStruct((ROWS, HID), BF16),
            jax.ShapeDtypeStruct((LOCAL, EMB, ROWS), BF16),
            jax.ShapeDtypeStruct((1, HID), F32),
            jax.ShapeDtypeStruct((1, HID), F32),
            jax.ShapeDtypeStruct((1, EMB), F32),
        ),
        in_specs=[hbm] * 7,
        out_specs=(vmem,) * 6,
        scratch_shapes=[
            pltpu.VMEM((FEAT, HID), BF16),
            pltpu.VMEM((ROWS, FEAT), BF16),
            pltpu.VMEM((ROWS, FEAT), BF16),
            pltpu.VMEM((SLOTS, RB, EMB), BF16),
            pltpu.VMEM((NC, RB, CH), BF16),
            pltpu.VMEM((NC, RB, CH), BF16),
            pltpu.VMEM((ROWS, HID), F32),
            pltpu.VMEM((ROWS, HID), F32),
            pltpu.VMEM((ROWS, HID), BF16),
            pltpu.VMEM((TAB, EMB, ROWS), BF16),
            pltpu.VMEM((4, TAB // 2, EB, ROWS), BF16),
            pltpu.VMEM((TAB // 2, EB, EMB), BF16),
            pltpu.VMEM((TAB // 2, EB, EMB), BF16),
            pltpu.VMEM((TAB, EB, EMB), BF16),
            pltpu.VMEM((TAB, EB, EMB), BF16),
            pltpu.VMEM((TAB // 2, EB, ROWS), BF16),
            pltpu.VMEM((TAB // 2, EB, ROWS), BF16),
            pltpu.VMEM((TAB // 2, EB, ROWS), BF16),
            pltpu.VMEM((TAB, EB, ROWS), BF16),
            pltpu.VMEM((TAB, EB, ROWS), BF16),
            pltpu.VMEM((TAB + 1, EB, ROWS), BF16),
            pltpu.VMEM((SLOTS, EB, ROWS), BF16),
            pltpu.VMEM((LOCAL, EMB, ROWS), BF16),
            pltpu.VMEM((1, ROWS), F32),
            pltpu.VMEM((NT, 1, ROWS), F32),
            pltpu.VMEM((1, ROWS), F32),
            pltpu.VMEM((NT, 1, ROWS), F32),
            pltpu.VMEM((1, ROWS), F32),
            pltpu.VMEM((NC, 1, ROWS), F32),
            pltpu.VMEM((1, HID), BF16),
            pltpu.VMEM((1, HID), BF16),
            pltpu.VMEM((1, ROWS), jnp.int32),
            pltpu.SMEM((TAB,), jnp.int32),
            pltpu.SMEM((NC,), jnp.int32),
            pltpu.VMEM((SLOTS, EMB), jnp.int32),
            pltpu.SMEM((SLOTS, EMB), jnp.int32),
            pltpu.SemaphoreType.REGULAR, pltpu.SemaphoreType.REGULAR,
            dma((6,)), dma,
            dma((NT,)), dma,
            tree, tree,
            dma((NCHUNK,)), dma,
            dma((NC,)), dma,
            tree, tree,
            dma((NT,)), dma,
            dma((NT,)), dma,
            dma((NC,)), dma,
            tree, tree,
            dma((NT,)), dma,
        ],
        compiler_params=pltpu.CompilerParams(
            collective_id=0, has_side_effects=True, vmem_limit_bytes=40 * 1024 * 1024
        ),
    )(
        *(
            pltpu.with_memory_space_constraint(v, pltpu.HBM)
            for v in (
                slot_of_table, partner, labels.reshape(1, ROWS), jnp.transpose(pooled, (1, 0, 2)),
                w_first.reshape(FEAT, HID), b_first, w_head,
            )
        )
    )
    pg, gf, gb, gh, loss = pl.pallas_call(
        finish,
        out_shape=(
            jax.ShapeDtypeStruct((LOCAL, EMB, ROWS), BF16),
            jax.ShapeDtypeStruct((FEAT, HID), BF16),
            jax.ShapeDtypeStruct((1, HID), F32),
            jax.ShapeDtypeStruct((1, HID), F32),
            jax.ShapeDtypeStruct((1,), F32),
        ),
        in_specs=[vmem] * 6,
        out_specs=(hbm, hbm, vmem, vmem, smem),
        scratch_shapes=[pltpu.VMEM((FEAT, HID), BF16), dma((NCHUNK,)), dma],
        compiler_params=pltpu.CompilerParams(vmem_limit_bytes=24 * 1024 * 1024),
    )(*results)
    return pg, gf[None], gb, gh, loss


def solution(mesh):
    in_specs = (
        P("copy", "table", None), P(), P(), P("copy"), P("copy", None, "table"), P("copy", "table"), P("copy", "table"),
    )
    out_specs = (
        P("table", None, "copy"), P("copy", None, "table"), P("copy", "table"), P("copy", "table"), P("copy"),
    )
    return jax.shard_map(on_device, mesh=mesh, in_specs=in_specs, out_specs=out_specs, check_vma=False)
```

```python
import jax
import jax.numpy as jnp
from jax import lax
from jax.experimental import pallas as pl
from jax.experimental.pallas import tpu as pltpu
from jax.sharding import PartitionSpec as P

MESH = pl.DeviceIdType.MESH
F32, BF16 = jnp.float32, jnp.bfloat16
NT, NC = 8, 32
TAB, EMB, SLOTS, LOCAL = 26, 128, 40, 5
ROWS, HID, FEAT = 256, 512, 3328
RB = ROWS // NT
EB = EMB // NT
CH = 256
NCHUNK = FEAT // CH
HALF = FEAT // 2

A, B, BOTH = (0, RB // 2), (RB // 2, RB // 2), (0, RB)
ALL, LOW, HIGH = (0, FEAT), (0, HALF), (HALF, HALF)
TREE = (
    ((0, 0), (0, 1), A, ALL, "y"),
    ((0, 0), (0, 1), B, ALL, "y"),
    ((0, 0), (3, 0), BOTH, ALL, "right"),
    ((0, 0), (1, 0), BOTH, ALL, "left"),
    ((0, 1), (3, 1), A, ALL, "right"),
    ((0, 1), (1, 1), A, ALL, "left"),
    ((3, 0), (2, 0), BOTH, LOW, "right"),
    ((1, 0), (2, 0), BOTH, HIGH, "left"),
    ((3, 0), (3, 1), B, ALL, "y"),
    ((1, 0), (1, 1), B, ALL, "y"),
    ((3, 1), (2, 1), A, LOW, "right"),
    ((1, 1), (2, 1), A, HIGH, "left"),
    ((2, 0), (2, 1), B, ALL, "y"),
)
TREE_STEPS = (((), (0, 2, 3, 1)), ((0,), (4, 5)), ((2,), (6, 8)), ((3,), (7, 9)), ((4,), (10,)), ((5,), (11,)), ((6, 7), (12,)),
              ((1, 8, 9, 10, 11, 12), ()))


def relay_copy(r):
    return 2 * (r + jnp.where(r >= 5, 1, 0) + jnp.where(r >= 9, 1, 0))


def kernel(
    slot_h, partner_h, labels_h, pooled, w_hbm, b_h, h_h,
    ft_out, low_out, pg_out, gb_out, gh_out, loss_out,
    w_v, feat, feat_t, by_slot, relay_in, relay_out, act_v, a32_v, low_v, gt_v, in_b, in_a1, in_a2, in_low, in_high, in_al, in_ar,
    in_ay, in_l, in_r, sums, placed, pg_in,
    z_own, z_in, q_own, q_in, qs_own, qs_in, b_v, h_v, y_v, slot_s, partner_s, inv_v, inv_s,
    in_sem, go_sem, load_sem, inv_sem,
    a_send, a_recv, ag_send, ag_recv, c_send, c_recv, d_send, d_recv, tg_send, tg_recv,
    l_send, l_recv, m_send, m_recv, t_send, t_recv, r_send, r_recv, z_send, z_recv,
):
    c = lax.axis_index("copy")
    k = lax.axis_index("table")
    x, y = lax.rem(k, 4), k // 4
    my_rows = pl.ds(pl.multiple_of(k * RB, RB), RB)
    chip = c // 2
    is_relay = (lax.rem(c, 2) == 0) & (chip != 5) & (chip != 10) & (chip != 15)
    my_r = jnp.where(is_relay, chip - jnp.where(chip >= 5, 1, 0) - jnp.where(chip >= 10, 1, 0), 0)

    barrier = pltpu.get_barrier_semaphore()

    is_gate = k == 0

    def signal(sem, copy, table):
        pl.semaphore_signal(sem, inc=1, device_id=(copy, table), device_id_type=MESH)

    def greet_table(d, _):
        j = lax.rem(k + d, NT)

        @pl.when(j != 0)
        def _():
            signal(barrier, c, j)

        return 0

    lax.fori_loop(1, NT, greet_table, 0)

    loads = [
        pltpu.make_async_copy(src, dst, load_sem.at[i])
        for i, (src, dst) in enumerate(
            ((slot_h, slot_s), (partner_h, partner_s), (labels_h, y_v), (b_h, b_v), (h_h, h_v), (w_hbm, w_v))
        )
    ]
    for load in loads:
        load.start()

    @pl.when(jnp.logical_not(is_gate))
    def _():
        pl.semaphore_wait(barrier, NT - 1)
        signal(in_sem, c, 0)

    @pl.when(is_gate)
    def _():
        pl.semaphore_wait(in_sem, NT - 1)

        def greet_copy(d, _):
            signal(barrier, lax.rem(c + d, NC), k)
            return 0

        lax.fori_loop(1, NC, greet_copy, 0)

    def all_in():
        @pl.when(is_gate)
        def _():
            pl.semaphore_wait(barrier, NC - 1)
            for j in range(1, NT):
                signal(go_sem, c, j)

        @pl.when(jnp.logical_not(is_gate))
        def _():
            pl.semaphore_wait(go_sem, 1)

    def remote(src, dst, send, recv, copy, table):
        return pltpu.make_async_remote_copy(
            src_ref=src, dst_ref=dst, send_sem=send, recv_sem=recv, device_id=(copy, table), device_id_type=MESH
        )

    def over_table(fn):
        def body(d, _):
            fn(d, lax.rem(k + d, NT))
            return 0

        lax.fori_loop(1, NT, body, 0)

    def take(ref, sem):
        pltpu.make_async_copy(ref, ref, sem).wait()

    def share(step):
        return lax.rem(y + step[1], 2) * 4 + lax.rem(x + step[0], 4)

    target = {"y": share((0, 1)), "right": share((1, 0)), "left": share((3, 0))}

    def region(buf, origin, rows, cols):
        first = pl.multiple_of(share(origin) * RB + rows[0], RB // 2)
        return buf.at[pl.ds(first, rows[1]), pl.ds(cols[0], cols[1])]

    def tree_copy(buf, send, recv, i):
        origin, _, rows, cols, to = TREE[i]
        piece = region(buf, origin, rows, cols)
        return remote(piece, piece, send.at[i], recv.at[i], c, target[to])

    def tree_step(buf, send, recv, step):
        waits, starts = TREE_STEPS[step]
        for i in waits:
            _, origin, rows, cols, _ = TREE[i]
            take(region(buf, origin, rows, cols), recv.at[i])
        for i in starts:
            tree_copy(buf, send, recv, i).start()

    def a_copy(d, j):
        rows = pl.ds(pl.multiple_of(j * RB, RB), RB)
        return remote(pooled.at[:, rows, :], by_slot.at[pl.ds(k * LOCAL, LOCAL)], a_send.at[d], a_recv, c, j)

    over_table(lambda d, j: a_copy(d, j).start())
    pltpu.make_async_copy(pooled.at[:, my_rows, :], by_slot.at[pl.ds(k * LOCAL, LOCAL)], a_recv).start()
    for load in loads:
        load.wait()

    lane = lax.broadcasted_iota(jnp.int32, (8, EMB), 1)
    slots = jnp.full((8, EMB), SLOTS, jnp.int32)
    for t in range(TAB):
        slots = jnp.where(lane == t, slot_s[t], slots)
    for i in range(SLOTS // 8):
        found = jnp.where(lax.broadcasted_iota(jnp.int32, (8, EMB), 0) + 8 * i == slots, lane, TAB)
        inv_v[8 * i : 8 * i + 8, :] = jnp.broadcast_to(jnp.min(found, axis=1, keepdims=True), (8, EMB))
    inv_copy = pltpu.make_async_copy(inv_v, inv_s, inv_sem)
    inv_copy.start()

    take(by_slot, a_recv)
    for t in range(TAB):
        feat[my_rows, t * EMB : (t + 1) * EMB] = by_slot[slot_s[t]]

    tree_step(feat, ag_send, ag_recv, 0)

    def c_copy(i):
        r = lax.rem(i + my_r, NCHUNK)
        to = relay_copy(r)
        src = feat.at[my_rows, pl.ds(pl.multiple_of(r * CH, CH), CH)]
        return src, to, remote(src, relay_in.at[c], c_send.at[i], c_recv, to, k)

    def c_start(i, _):
        src, to, copy = c_copy(i)

        @pl.when(to != c)
        def _():
            copy.start()

        @pl.when(to == c)
        def _():
            pltpu.make_async_copy(src, relay_in.at[c], c_recv).start()

        return 0

    all_in()
    lax.fori_loop(0, NCHUNK, c_start, 0)
    for step in range(1, 7):
        tree_step(feat, ag_send, ag_recv, step)

    my_cols = pl.ds(pl.multiple_of(my_r * CH, CH), CH)

    def d_copy(d, p):
        return remote(relay_out.at[p], feat_t.at[my_rows, my_cols], d_send.at[d], d_recv, p, k)

    @pl.when(is_relay)
    def _():
        take(relay_in, c_recv)

        def pick(p, _):
            relay_out[p] = relay_in[partner_s[p]]
            return 0

        lax.fori_loop(0, NC, pick, 0, unroll=4)

        def d_start(d, _):
            d_copy(d, lax.rem(c + d, NC)).start()
            return 0

        lax.fori_loop(1, NC, d_start, 0)
        pltpu.make_async_copy(relay_out.at[c], feat_t.at[my_rows, my_cols], d_recv).start()

    tree_step(feat, ag_send, ag_recv, 7)

    def head_row(total):
        return jnp.sum(jnp.transpose(total), axis=0, keepdims=True)

    total = jnp.zeros((ROWS, EMB), F32)
    for n in range(HID // CH):
        cols = slice(n * CH, (n + 1) * CH)
        head = h_v[:, cols].astype(F32)
        pre = jnp.dot(feat[...], w_v[:, cols], preferred_element_type=F32) + b_v[:, cols].astype(F32)
        sig = jax.nn.sigmoid(pre)
        act = pre * sig
        act_v[:, cols] = act
        a32 = head * (sig * (1.0 + pre * (1.0 - sig)))
        a32_v[:, cols] = a32
        low_v[:, cols] = a32.astype(BF16)
        weighed = act * head
        total = total + (weighed[:, :EMB] + weighed[:, EMB:])
    z_own[...] = head_row(total)

    z_in[k] = z_own[...]

    def l_copy(d, j):
        return remote(z_own, z_in.at[k], l_send.at[d], l_recv, c, j)

    over_table(lambda d, j: l_copy(d, j).start())

    def partials():
        def gt_step(i, _):
            rows = pl.ds(pl.multiple_of(i * CH, CH), CH)
            g = lax.dot_general(w_v[rows, :], low_v[...], (((1,), (1,)), ((), ())), preferred_element_type=F32)
            gt_v[pl.ds(i * 2, 2)] = g.astype(BF16).reshape(2, EMB, ROWS)
            return 0

        lax.fori_loop(0, NCHUNK, gt_step, 0)

    def part(step, tables=(0, TAB), lanes=(0, ROWS)):
        first = pl.multiple_of(share(step) * EB, EB)
        return pl.ds(tables[0], tables[1]), pl.ds(first, EB), pl.ds(lanes[0], lanes[1])

    ta, tb, every = (0, TAB // 2), (TAB // 2, TAB // 2), (0, TAB)
    low, high, full = (0, EMB), (EMB, EMB), (0, ROWS)
    messages = (
        ((2, 1), tb, full, in_b.at[0], "y"),
        ((2, 1), ta, low, in_a1, "left"),
        ((2, 1), ta, high, in_a2, "right"),
        ((3, 1), tb, full, in_b.at[1], "y"),
        ((1, 1), tb, full, in_b.at[2], "y"),
        ((0, 1), tb, full, in_b.at[3], "y"),
        ((2, 0), every, low, in_low, "left"),
        ((2, 0), every, high, in_high, "right"),
        ((3, 1), ta, full, in_al, "left"),
        ((1, 1), ta, full, in_ar, "right"),
        ((3, 0), every, full, in_l, "left"),
        ((1, 0), every, full, in_r, "right"),
        ((0, 1), ta, full, in_ay, "y"),
    )

    def reduce_copy(i):
        step, tables, lanes, dst, to = messages[i]
        return remote(gt_v.at[part(step, tables, lanes)], dst, r_send.at[i], r_recv.at[i], c, target[to])

    def add(step, tables, lanes, *arrived):
        where = part(step, tables, lanes)
        total = gt_v[where].astype(F32)
        for ref, i in arrived:
            take(ref, r_recv.at[i])
            total = total + ref[...].astype(F32)
        gt_v[where] = total.astype(BF16)

    def reduce_leaves():
        for i in range(6):
            reduce_copy(i).start()

    def reduce_first():
        add((2, 0), tb, full, (in_b.at[0], 0))
        reduce_copy(6).start()
        reduce_copy(7).start()
        add((3, 1), ta, low, (in_a1, 1))
        reduce_copy(8).start()
        add((1, 1), ta, high, (in_a2, 2))
        reduce_copy(9).start()

    def reduce_second():
        add((3, 0), tb, full, (in_b.at[1], 3))
        add((3, 0), every, low, (in_low, 6))
        reduce_copy(10).start()
        add((1, 0), tb, full, (in_b.at[2], 4))
        add((1, 0), every, high, (in_high, 7))
        reduce_copy(11).start()
        add((0, 1), ta, full, (in_al, 8), (in_ar, 9))
        reduce_copy(12).start()

    ahead = c < NC // 2
    behind = jnp.logical_not(ahead)

    @pl.when(ahead)
    def _():
        partials()
        reduce_leaves()

    take(feat_t.at[my_rows], d_recv)
    tree_step(feat_t, tg_send, tg_recv, 0)

    @pl.when(ahead)
    def _():
        reduce_first()

    @pl.when(behind)
    def _():
        partials()


    for step in range(1, 7):
        tree_step(feat_t, tg_send, tg_recv, step)

    @pl.when(behind)
    def _():
        reduce_leaves()

    def teacher(half):
        rows = pl.ds(pl.multiple_of(half * EMB, EMB), EMB)
        total = jnp.zeros((EMB, EMB), F32)
        for n in range(HID // CH):
            cols = slice(n * CH, (n + 1) * CH)
            pre = jnp.dot(feat_t[rows, :], w_v[:, cols], preferred_element_type=F32) + b_v[:, cols].astype(F32)
            weighed = pre * jax.nn.sigmoid(pre) * h_v[:, cols].astype(F32)
            total = total + (weighed[:, :EMB] + weighed[:, EMB:])
        q_own[:, rows] = head_row(total)

    teacher(y)
    tree_step(feat_t, tg_send, tg_recv, 7)
    @pl.when(behind)
    def _():
        reduce_first()

    teacher(1 - y)
    q_in[k] = q_own[...]

    def m_copy(d, j):
        return remote(q_own, q_in.at[k], m_send.at[d], m_recv, c, j)

    over_table(lambda d, j: m_copy(d, j).start())

    reduce_second()


    take(z_in.at[pl.ds(0, NT - 1)], l_recv)
    take(q_in.at[pl.ds(0, NT - 1)], m_recv)
    qs_own[...] = jnp.sum(q_in[...], axis=0)
    qs_in[c] = qs_own[...]

    def t_copy(d):
        return remote(qs_own, qs_in.at[c], t_send.at[d], t_recv, lax.rem(c + d, NC), k)

    def t_start(d, _):
        t_copy(d).start()
        return 0

    lax.fori_loop(1, NC, t_start, 0)


    for ref, i in ((in_b.at[3], 5), (in_l, 10), (in_r, 11), (in_ay, 12)):
        take(ref, r_recv.at[i])
    inv_copy.wait()
    mine = pl.ds(pl.multiple_of(k * EB, EB), EB)
    half = TAB // 2
    total = gt_v[0:half, mine, :].astype(F32) + in_ay[...].astype(F32)
    total = total + in_l[0:half].astype(F32) + in_r[0:half].astype(F32)
    sums[0:half] = total.astype(BF16)
    total = gt_v[half:TAB, mine, :].astype(F32) + in_b[3].astype(F32)
    total = total + in_l[half:TAB].astype(F32) + in_r[half:TAB].astype(F32)
    sums[half:TAB] = total.astype(BF16)
    sums[TAB] = jnp.zeros((EB, ROWS), BF16)

    def place(s, _):
        placed[s] = sums[inv_s[s, 0]]
        return 0

    lax.fori_loop(0, SLOTS, place, 0, unroll=4)

    def z_copy(d, j):
        return remote(placed.at[pl.ds(j * LOCAL, LOCAL)], pg_in.at[:, mine, :], z_send.at[d], z_recv, c, j)

    over_table(lambda d, j: z_copy(d, j).start())
    pltpu.make_async_copy(placed.at[pl.ds(k * LOCAL, LOCAL)], pg_in.at[:, mine, :], z_recv).start()

    def flip(i, _):
        rows = pl.ds(pl.multiple_of(i * CH, CH), CH)
        ft_out[rows, :] = jnp.transpose(feat[:, rows])
        return 0

    lax.fori_loop(0, NCHUNK, flip, 0)

    over_table(lambda d, j: a_copy(d, j).wait_send())

    def c_wait(i, _):
        _, to, copy = c_copy(i)

        @pl.when(to != c)
        def _():
            copy.wait_send()

        return 0

    lax.fori_loop(0, NCHUNK, c_wait, 0)
    for i in range(len(TREE)):
        tree_copy(feat, ag_send, ag_recv, i).wait_send()
        tree_copy(feat_t, tg_send, tg_recv, i).wait_send()

    @pl.when(is_relay)
    def _():
        def d_wait(d, _):
            d_copy(d, lax.rem(c + d, NC)).wait_send()
            return 0

        lax.fori_loop(1, NC, d_wait, 0)

    def t_wait(d, _):
        t_copy(d).wait_send()
        return 0

    lax.fori_loop(1, NC, t_wait, 0)

    def rest(d, j):
        l_copy(d, j).wait_send()
        m_copy(d, j).wait_send()
        z_copy(d, j).wait_send()

    over_table(rest)
    for i in range(len(messages)):
        reduce_copy(i).wait_send()

    take(qs_in.at[pl.ds(0, NC - 1)], t_recv)
    z = jnp.sum(z_in[...], axis=0)
    q = jax.nn.sigmoid(qs_in[partner_s[c]])
    target_y = y_v[...].astype(F32)
    soft = jnp.maximum(z, 0.0) + jnp.log1p(jnp.exp(-jnp.abs(z)))
    lg = 2.0 * jax.nn.sigmoid(z) - target_y - q
    loss_out[...] = jnp.broadcast_to(
        jnp.sum(2.0 * soft - target_y * z - q * z, axis=1, keepdims=True) * (1.0 / ROWS), (1, EMB)
    )
    lg_col = jnp.transpose(jnp.broadcast_to(lg, (EMB, ROWS)))
    for n in range(HID // EMB):
        cols = slice(n * EMB, (n + 1) * EMB)
        grad_pre = lg_col * a32_v[:, cols]
        low_out[:, cols] = grad_pre.astype(BF16)
        gb_out[:, cols] = jnp.sum(grad_pre, axis=0, keepdims=True)
        gh_out[:, cols] = jnp.sum(lg_col * act_v[:, cols], axis=0, keepdims=True)

    take(pg_in, z_recv)
    for e in range(LOCAL):
        pg_out[e] = (pg_in[e].astype(F32) * lg).astype(BF16)


def finish(ft_v, low_v, pg_v, gb_v, gh_v, loss_v, pg_out, gf_out, gb_out, gh_out, loss_out, gf_v, gf_sem, pg_sem):
    pg_copy = pltpu.make_async_copy(pg_v, pg_out, pg_sem)
    pg_copy.start()
    copies = []
    for i in range(NCHUNK):
        rows = pl.ds(i * CH, CH)
        gf_v[rows, :] = jnp.dot(ft_v[rows, :], low_v[...], preferred_element_type=F32).astype(BF16)
        copy = pltpu.make_async_copy(gf_v.at[rows], gf_out.at[rows], gf_sem.at[i])
        copy.start()
        copies.append(copy)
    gb_out[...] = gb_v[...]
    gh_out[...] = gh_v[...]
    loss_out[0] = jnp.sum(loss_v[:, 0:1])
    pg_copy.wait()
    for copy in copies:
        copy.wait()


def on_device(pooled, slot_of_table, partner, labels, w_first, b_first, w_head):
    vmem = pl.BlockSpec(memory_space=pltpu.VMEM)
    smem = pl.BlockSpec(memory_space=pltpu.SMEM)
    hbm = pl.BlockSpec(memory_space=pltpu.HBM)
    dma = pltpu.SemaphoreType.DMA
    tree = dma((len(TREE),))
    results = pl.pallas_call(
        kernel,
        out_shape=(
            jax.ShapeDtypeStruct((FEAT, ROWS), BF16),
            jax.ShapeDtypeStruct((ROWS, HID), BF16),
            jax.ShapeDtypeStruct((LOCAL, EMB, ROWS), BF16),
            jax.ShapeDtypeStruct((1, HID), F32),
            jax.ShapeDtypeStruct((1, HID), F32),
            jax.ShapeDtypeStruct((1, EMB), F32),
        ),
        in_specs=[hbm] * 7,
        out_specs=(vmem,) * 6,
        scratch_shapes=[
            pltpu.VMEM((FEAT, HID), BF16),
            pltpu.VMEM((ROWS, FEAT), BF16),
            pltpu.VMEM((ROWS, FEAT), BF16),
            pltpu.VMEM((SLOTS, RB, EMB), BF16),
            pltpu.VMEM((NC, RB, CH), BF16),
            pltpu.VMEM((NC, RB, CH), BF16),
            pltpu.VMEM((ROWS, HID), F32),
            pltpu.VMEM((ROWS, HID), F32),
            pltpu.VMEM((ROWS, HID), BF16),
            pltpu.VMEM((TAB, EMB, ROWS), BF16),
            pltpu.VMEM((4, TAB // 2, EB, ROWS), BF16),
            pltpu.VMEM((TAB // 2, EB, EMB), BF16),
            pltpu.VMEM((TAB // 2, EB, EMB), BF16),
            pltpu.VMEM((TAB, EB, EMB), BF16),
            pltpu.VMEM((TAB, EB, EMB), BF16),
            pltpu.VMEM((TAB // 2, EB, ROWS), BF16),
            pltpu.VMEM((TAB // 2, EB, ROWS), BF16),
            pltpu.VMEM((TAB // 2, EB, ROWS), BF16),
            pltpu.VMEM((TAB, EB, ROWS), BF16),
            pltpu.VMEM((TAB, EB, ROWS), BF16),
            pltpu.VMEM((TAB + 1, EB, ROWS), BF16),
            pltpu.VMEM((SLOTS, EB, ROWS), BF16),
            pltpu.VMEM((LOCAL, EMB, ROWS), BF16),
            pltpu.VMEM((1, ROWS), F32),
            pltpu.VMEM((NT, 1, ROWS), F32),
            pltpu.VMEM((1, ROWS), F32),
            pltpu.VMEM((NT, 1, ROWS), F32),
            pltpu.VMEM((1, ROWS), F32),
            pltpu.VMEM((NC, 1, ROWS), F32),
            pltpu.VMEM((1, HID), BF16),
            pltpu.VMEM((1, HID), BF16),
            pltpu.VMEM((1, ROWS), jnp.int32),
            pltpu.SMEM((TAB,), jnp.int32),
            pltpu.SMEM((NC,), jnp.int32),
            pltpu.VMEM((SLOTS, EMB), jnp.int32),
            pltpu.SMEM((SLOTS, EMB), jnp.int32),
            pltpu.SemaphoreType.REGULAR, pltpu.SemaphoreType.REGULAR,
            dma((6,)), dma,
            dma((NT,)), dma,
            tree, tree,
            dma((NCHUNK,)), dma,
            dma((NC,)), dma,
            tree, tree,
            dma((NT,)), dma,
            dma((NT,)), dma,
            dma((NC,)), dma,
            tree, tree,
            dma((NT,)), dma,
        ],
        compiler_params=pltpu.CompilerParams(
            collective_id=0, has_side_effects=True, vmem_limit_bytes=40 * 1024 * 1024
        ),
    )(
        *(
            pltpu.with_memory_space_constraint(v, pltpu.HBM)
            for v in (
                slot_of_table, partner, labels.reshape(1, ROWS), jnp.transpose(pooled, (1, 0, 2)),
                w_first.reshape(FEAT, HID), b_first, w_head,
            )
        )
    )
    pg, gf, gb, gh, loss = pl.pallas_call(
        finish,
        out_shape=(
            jax.ShapeDtypeStruct((LOCAL, EMB, ROWS), BF16),
            jax.ShapeDtypeStruct((FEAT, HID), BF16),
            jax.ShapeDtypeStruct((1, HID), F32),
            jax.ShapeDtypeStruct((1, HID), F32),
            jax.ShapeDtypeStruct((1,), F32),
        ),
        in_specs=[vmem] * 6,
        out_specs=(hbm, hbm, vmem, vmem, smem),
        scratch_shapes=[pltpu.VMEM((FEAT, HID), BF16), dma((NCHUNK,)), dma],
        compiler_params=pltpu.CompilerParams(vmem_limit_bytes=24 * 1024 * 1024),
    )(*results)
    return pg, gf[None], gb, gh, loss


def solution(mesh):
    in_specs = (
        P("copy", "table", None), P(), P(), P("copy"), P("copy", None, "table"), P("copy", "table"), P("copy", "table"),
    )
    out_specs = (
        P("table", None, "copy"), P("copy", None, "table"), P("copy", "table"), P("copy", "table"), P("copy"),
    )
    return jax.shard_map(on_device, mesh=mesh, in_specs=in_specs, out_specs=out_specs, check_vma=False)
```
